768 devices in a mesh: seq: 12 (over z), head: 64 (over x, y, core).
Axes of the slice: x: 4, y: 8, z: 12, core: 2. Of those that a mesh axis runs over, the one named last changes fastest.
Arguments:
- x_in: bfloat16 [6144, 8192], P('seq', 'head'), may hold values from -6 to 6
- gate_in: bfloat16 [6144, 8192], P('seq', 'head'), may hold values from -6 to 6
- b_in: bfloat16 [6144, 128], P('seq'), may hold values from -6 to 6
- c_in: bfloat16 [6144, 128], P('seq'), may hold values from -0.078125 to 0.078125
- log_decay: float32 [128, 6144], P('head', 'seq'), may hold values from -1 to 0
- w_out: bfloat16 [8192, 8192], P(None, 'head'), may hold values from -0.1875 to 0.1875
Outputs:
- mixed: bfloat16 [6144, 8192], P('seq', 'head')
The draws below stay inside these ranges and needn't reach their ends.
All inputs are finite; a program needn't handle non-finite values.
Results may differ from the reference program's by a relative error of at most 0.0064.
Values may be sent and summed in bfloat16 or wider, within the bound.
A program may use at most 64 MiB of HBM per device.

```python
import math
import jax
import jax.numpy as jnp
from jax import lax

WIDTH = 8192
NUM_GATED_UNITS = 128
HEAD_SIZE = 64
STATE = 128
GROUP = 256
TOK_DEV = 512
SEQUENCE_LENGTH = 6144
INNER = 8192


def draw_log_decay(key, part):
    lookup_matrix_lines = jax.random.split(key, 6)
    slow_count = NUM_GATED_UNITS // 2
    order = jax.random.permutation(lookup_matrix_lines[0], NUM_GATED_UNITS)
    gradual_amplitude = order < slow_count
    unit = jax.random.uniform(lookup_matrix_lines[1], (NUM_GATED_UNITS,), jnp.float32)
    slow_rate = jnp.exp(math.log(0.1) + unit * math.log(4.0)) / SEQUENCE_LENGTH
    fast_rate = jnp.exp(math.log(1.0 / 50.0) + unit * math.log(50.0 / 30.0))
    rate = jnp.where(gradual_amplitude, slow_rate, fast_rate)
    factor = jnp.exp(jax.random.uniform(lookup_matrix_lines[2], (NUM_GATED_UNITS, SEQUENCE_LENGTH), jnp.float32, -math.log(2.0), math.log(2.0)))
    block_factor = jnp.exp(jax.random.uniform(lookup_matrix_lines[3], (NUM_GATED_UNITS, SEQUENCE_LENGTH // TOK_DEV), jnp.float32, -math.log(2.0), math.log(2.0)))
    block_factor = jnp.repeat(block_factor, TOK_DEV, axis=1)
    dispersion_amplitude = rate[:, None] * factor * block_factor
    places = jax.random.randint(lookup_matrix_lines[4], (3,), 0, SEQUENCE_LENGTH)
    impact_amplitude = jnp.any(jnp.arange(SEQUENCE_LENGTH)[None, :] == places[:, None], axis=0)
    sudden_amplitude = jnp.exp(jax.random.uniform(lookup_matrix_lines[5], (NUM_GATED_UNITS, SEQUENCE_LENGTH), jnp.float32, math.log(0.22), math.log(0.69)))
    payload_matrix_lines = jnp.where(gradual_amplitude[:, None] & impact_amplitude[None, :], sudden_amplitude, dispersion_amplitude)
    return -payload_matrix_lines


def raised(array, key, source, target, shards_of, factor):
    def block_of(dim):
        return (jnp.arange(array.shape[dim]) // (array.shape[dim] // shards_of)).reshape((-1,) + (1,) * (array.ndim - 1 - dim))

    first = jax.random.permutation(key, shards_of)[block_of(target)]
    far = (block_of(target) + shards_of // 2) % shards_of
    return jnp.where((block_of(source) == first) | (block_of(source) == far), factor * array, array)


def level_of(stream_key, dims, cuts, least, largest):
    level, own = 1.0, jax.random.fold_in(stream_key, 6)
    for dim, shards_of in cuts:
        draws = jnp.exp(jax.random.uniform(jax.random.fold_in(own, dim), (shards_of,), jnp.float32, least / len(cuts), largest / len(cuts)))
        level = level * jnp.repeat(draws, dims[dim] // shards_of).reshape([-1 if axis == dim else 1 for axis in range(len(dims))])
    return level


def scatter_about(own_key, extent, scale, reach, cuts=(), held_as=jnp.bfloat16):
    entries = scale * jax.random.normal(own_key, extent, jnp.float32)
    if cuts:
        entries = entries * level_of(own_key, extent, cuts, -0.22, 0.18)
    return jnp.clip(entries, -reach, reach).astype(held_as)


def bell_draw_with(own_key, dims, width, bound, cuts, heavy, held_as=jnp.bfloat16):
    values = width * jax.random.normal(own_key, dims, jnp.float32)
    if cuts:
        values = values * level_of(own_key, dims, cuts, -0.22, 0.18)
    return jnp.clip(raised(values, jax.random.fold_in(own_key, 3), *heavy), -bound, bound).astype(held_as)


def setup_inputs(seed: int = 0) -> dict:
    seeds = jax.random.split(jax.random.key(seed), 7)
    return {
        "x_in": scatter_about(seeds[0], (SEQUENCE_LENGTH, INNER), 1.0, 6.0, ((0, 12), (1, 64))),
        "gate_in": scatter_about(seeds[1], (SEQUENCE_LENGTH, INNER), 1.0, 6.0, ((0, 12), (1, 64))),
        "b_in": scatter_about(seeds[2], (SEQUENCE_LENGTH, STATE), 1.0, 6.0, ((0, 12),)),
        "c_in": scatter_about(seeds[3], (SEQUENCE_LENGTH, STATE), ((STATE * GROUP) ** -0.5), 0.078125, ((0, 12),)),
        "log_decay": draw_log_decay(jax.random.fold_in(seeds[6], 71), 0),
        "w_out": bell_draw_with(seeds[5], (INNER, WIDTH), INNER ** -0.5, 0.1875, ((1, 64),), (0, 1, 64, 4.0)),
    }


def reference(x_in, gate_in, b_in, c_in, log_decay, w_out):
    blocks = SEQUENCE_LENGTH // GROUP
    inputs_x = x_in.reshape(blocks, GROUP, NUM_GATED_UNITS, HEAD_SIZE)
    inputs_b = b_in.reshape(blocks, GROUP, STATE)
    inputs_c = c_in.reshape(blocks, GROUP, STATE)
    decays = log_decay.reshape(NUM_GATED_UNITS, blocks, GROUP).transpose(1, 0, 2)
    lower = jnp.tril(jnp.ones((GROUP, GROUP), dtype=bool))

    def advance(carried, pieces):
        x_blk, b_blk, c_blk, d_blk = pieces
        running = jnp.cumsum(d_blk, axis=1)
        scores = jnp.dot(c_blk, b_blk.T, preferred_element_type=jnp.float32)
        dispersion_amplitude = jnp.where(lower, running[:, :, None] - running[:, None, :], 0.0)
        weights = jnp.where(lower, scores[None] * jnp.exp(dispersion_amplitude), 0.0).astype(jnp.bfloat16)
        y_diag = jnp.einsum("hts,shp->thp", weights.astype(jnp.float32), x_blk.astype(jnp.float32))
        start_bf = carried.astype(jnp.bfloat16)
        y_carry = jnp.einsum("tn,hnp->thp", c_blk.astype(jnp.float32), start_bf.astype(jnp.float32))
        y_carry = y_carry * jnp.exp(running).T[:, :, None]
        to_end = jnp.exp(running[:, -1:] - running)
        b_scaled = (b_blk.astype(jnp.float32)[None] * to_end[:, :, None]).astype(jnp.bfloat16)
        local_state = jnp.einsum("htn,thp->hnp", b_scaled.astype(jnp.float32), x_blk.astype(jnp.float32))
        carried = carried * jnp.exp(running[:, -1])[:, None, None] + local_state
        return carried, y_diag + y_carry

    initial = jnp.zeros((NUM_GATED_UNITS, STATE, HEAD_SIZE), jnp.float32)
    final_state, outputs = lax.scan(advance, initial, (inputs_x, inputs_b, inputs_c, decays))
    mixed = outputs.reshape(SEQUENCE_LENGTH, NUM_GATED_UNITS * HEAD_SIZE)
    gated = (mixed * jax.nn.silu(gate_in.astype(jnp.float32))).astype(jnp.bfloat16)
    return jnp.dot(gated, w_out, preferred_element_type=jnp.float32).astype(jnp.bfloat16)
```

```python
import functools

import jax
import jax.numpy as jnp
from jax import lax
from jax.experimental import pallas as pl
from jax.experimental.pallas import tpu as pltpu
from jax.sharding import PartitionSpec as P

MESH = pl.DeviceIdType.MESH
BLOCK = 256
NX, NY, NC = 4, 8, 2
SPAN = 4
CHUNKS = 4
NT = (((1,), (1,)), ((), ()))
TN = (((0,), (0,)), ((), ()))
F32 = jnp.float32
BF16 = jnp.bfloat16


def exact(a, b):
    return lax.dot_general(a, b, NT, precision=lax.Precision.HIGHEST, preferred_element_type=F32)


def pack(ref, state, total):
    n = state.shape[0]
    row = lax.broadcasted_iota(jnp.int32, (16, state.shape[1]), 0)
    high = total.astype(BF16).astype(F32)
    tail = jnp.where(row == 0, high, jnp.where(row == 1, total - high, 0.0))
    ref[0:n, :] = state.astype(BF16)
    ref[n : n + 16, :] = tail.astype(BF16)


def unpack(ref, n):
    tail = ref[n : n + 16, :].astype(F32)
    return ref[0:n, :].astype(F32), tail[0:1] + tail[1:2]


def kernel(
    seq_size,
    x_ref,
    gate_ref,
    b_ref,
    c_ref,
    decay_ref,
    w_ref,
    out_ref,
    m1,
    m2,
    m2_in,
    diag,
    wide,
    blocks,
    w_buf,
    total,
    part,
    part_in,
    m1_s,
    m1_r,
    m2_s,
    m2_r,
    w_s,
    w_r,
    own_s,
    ring_s,
    ring_r,
    twin_s,
    twin_r,
    part_s,
    part_r,
):
    rows, columns = x_ref.shape
    states = b_ref.shape[1]
    channels = columns // decay_ref.shape[0]
    step = rows // CHUNKS
    s = lax.axis_index("seq")
    head = lax.axis_index("head")
    px, py, core = head // (NY * NC), (head // NC) % NY, head % NC
    group, place = s // SPAN, s % SPAN

    def device(z, x, y, c):
        return (z, (x * NY + y) * NC + c)

    mates = [(place + i) % SPAN for i in range(1, SPAN)]
    mate_ids = [device(group * SPAN + m, px, py, core) for m in mates]
    ahead_ids = [device((s + SPAN * i) % seq_size, px, py, core) for i in (1, 2)]
    peers = [(px + i) % NX for i in range(1, NX)]
    peer_ids = [device(s, p, py, core) for p in peers]
    up = device(s, px, (py + 1) % NY, core)
    down = device(s, px, (py + NY - 1) % NY, core)
    twin = device(s, px, py, 1 - core)

    def remote(src, dst, send, recv, to):
        return pltpu.make_async_remote_copy(
            src_ref=src, dst_ref=dst, send_sem=send, recv_sem=recv, device_id=to, device_id_type=MESH
        )

    partners = mate_ids + ahead_ids + peer_ids + [up, down, twin]
    barrier = pltpu.get_barrier_semaphore()
    for to in partners:
        pl.semaphore_signal(barrier, inc=1, device_id=to, device_id_type=MESH)

    depth = NY * NC * columns
    own_w = pltpu.make_async_copy(w_ref.at[pl.ds(px * depth, depth), :], w_buf.at[px], own_s)
    own_w.start()
    t_of = lax.broadcasted_iota(jnp.int32, (BLOCK, BLOCK), 0)
    s_of = lax.broadcasted_iota(jnp.int32, (BLOCK, BLOCK), 1)
    lower = s_of <= t_of
    ones = jnp.where(lower, 1.0, 0.0)
    first_head = lax.broadcasted_iota(jnp.int32, (BLOCK, columns), 1) < channels
    first_row = lax.broadcasted_iota(jnp.int32, (columns, BLOCK), 0) < channels
    local, cum_last = [], []
    for q in range(rows // BLOCK):
        at = slice(q * BLOCK, (q + 1) * BLOCK)
        decay = decay_ref[:, at]
        cum = exact(ones, jnp.where(first_row, decay[0:1], decay[1:2]))
        wide[at, :] = cum
        last = cum[BLOCK - 1 :, :]
        to_end = jnp.exp(last - cum)
        b = b_ref[at, :].astype(F32)
        x = x_ref[at, :]
        halves = [
            lax.dot_general(
                (b * to_end[:, h * channels : h * channels + 1]).astype(BF16),
                x,
                TN,
                preferred_element_type=F32,
            )
            for h in range(2)
        ]
        local.append(jnp.where(first_head[:states], halves[0], halves[1]))
        cum_last.append(last)
    m1_own = m1.at[place]
    pack(
        m1_own,
        local[0] * jnp.exp(cum_last[1]) + local[1],
        jnp.exp(cum_last[0] + cum_last[1]),
    )

    pl.semaphore_wait(barrier, len(partners))
    sent = []
    for i, to in enumerate(mate_ids):
        copy = remote(m1_own, m1_own, m1_s.at[i], m1_r.at[i], to)
        copy.start()
        sent.append(copy)
    for i, to in enumerate(peer_ids):
        copy = remote(
            w_ref.at[pl.ds(peers[i] * depth, depth), :], w_buf.at[px], w_s.at[i], w_r.at[i], to
        )
        copy.start()
        sent.append(copy)

    for q in range(rows // BLOCK):
        at = slice(q * BLOCK, (q + 1) * BLOCK)
        decay = decay_ref[:, at]
        cum = wide[at, :]
        x = x_ref[at, :]
        scores = lax.dot_general(c_ref[at, :], b_ref[at, :], NT, preferred_element_type=F32)
        along = exact(jnp.where(first_row[56:72], decay[0:1], decay[1:2]), ones)
        halves = []
        for h in range(2):
            gap = cum[:, h * channels : h * channels + 1] - along[8 * h : 8 * h + 1, :]
            weights = jnp.where(lower, scores * jnp.exp(jnp.where(lower, gap, 0.0)), 0.0)
            halves.append(jnp.dot(weights.astype(BF16), x, preferred_element_type=F32))
        diag[at, :] = jnp.where(first_head, halves[0], halves[1])

    for i in range(SPAN - 1):
        slot = m1.at[(place + SPAN - 1 - i) % SPAN]
        remote(slot, slot, m1_s.at[i], m1_r.at[i], mate_ids[i]).wait_recv()
    state = jnp.zeros((states, columns), F32)
    decayed = jnp.ones((1, columns), F32)
    before, before_decay = state, decayed
    for i in range(SPAN):
        before = jnp.where(place == i, state, before)
        before_decay = jnp.where(place == i, decayed, before_decay)
        more, its_decay = unpack(m1.at[i], states)
        state = state * its_decay + more
        decayed = decayed * its_decay
    pack(m2, state, decayed)
    for i, to in enumerate(ahead_ids):
        copy = remote(m2, m2_in.at[i], m2_s.at[i], m2_r.at[i], to)
        copy.start()
        sent.append(copy)
    for i, to in enumerate(ahead_ids):
        remote(m2, m2_in.at[i], m2_s.at[i], m2_r.at[i], to).wait_recv()
    near, near_decay = unpack(m2_in.at[0], states)
    far, _ = unpack(m2_in.at[1], states)
    earlier = jnp.where(group >= 2, far * near_decay, 0.0) + near
    start = before + jnp.where(group >= 1, earlier * before_decay, 0.0)
    starts = [start, start * jnp.exp(cum_last[0]) + local[0]]

    mine = py * NC + core
    for r in range(CHUNKS):
        at = slice(r * step, (r + 1) * step)
        start_bf = starts[r * step // BLOCK].astype(BF16)
        carry = jnp.dot(c_ref[at, :], start_bf, preferred_element_type=F32)
        y = diag[at, :] + carry * jnp.exp(wide[at, :])
        gate = gate_ref[at, :].astype(F32)
        blocks[mine, at, :] = (y * (gate / (1.0 + jnp.exp(-gate)))).astype(BF16)
        here = blocks.at[mine, at]
        for d, to in enumerate((up, down)):
            copy = remote(here, here, ring_s.at[r, d, 0], ring_r.at[r, d, 0], to)
            copy.start()
            sent.append(copy)
        copy = remote(here, here, twin_s.at[r, 0], twin_r.at[r, 0], twin)
        copy.start()
        sent.append(copy)

    def hops(r, d):
        return NY // 2 if (r + d) % 2 == 0 else NY // 2 - 1

    def behind(hop, d):
        return (py + NY - hop) % NY if d == 0 else (py + hop) % NY

    for hop in range(1, NY // 2 + 1):
        for r in range(CHUNKS):
            at = slice(r * step, (r + 1) * step)
            for d, to in enumerate((up, down)):
                if hop > hops(r, d):
                    continue
                here = blocks.at[behind(hop, d) * NC + core, at]
                remote(here, here, ring_s.at[r, d, hop - 1], ring_r.at[r, d, hop - 1], to).wait_recv()
                if hop < hops(r, d):
                    copy = remote(here, here, ring_s.at[r, d, hop], ring_r.at[r, d, hop], to)
                    copy.start()
                    sent.append(copy)
                which = 2 * hop - 1 + d if hop < NY // 2 else NY - 1
                copy = remote(here, here, twin_s.at[r, which], twin_r.at[r, which], twin)
                copy.start()
                sent.append(copy)

    own_w.wait()
    for i in range(NX - 1):
        slot = w_buf.at[(px + NX - 1 - i) % NX]
        remote(slot, slot, w_s.at[i], w_r.at[i], peer_ids[i]).wait_recv()
    for r in range(CHUNKS):
        at = slice(r * step, (r + 1) * step)
        for which in range(NY):
            if which == 0:
                where = py
            elif which < NY - 1:
                where = behind((which + 1) // 2, (which + 1) % 2)
            else:
                where = (py + NY // 2) % NY
            there = blocks.at[where * NC + 1 - core, at]
            remote(there, there, twin_s.at[r, which], twin_r.at[r, which], twin).wait_recv()
        gathered = jnp.concatenate([blocks[k, at, :] for k in range(NY * NC)], axis=1)
        for i, to in enumerate(peer_ids):
            part[i, at, :] = jnp.dot(
                gathered, w_buf[peers[i]], preferred_element_type=F32
            ).astype(BF16)
            copy = remote(part.at[i, at], part_in.at[i, at], part_s.at[i, r], part_r.at[i, r], to)
            copy.start()
            sent.append(copy)
        total[at, :] = jnp.dot(gathered, w_buf[px], preferred_element_type=F32)
    for r in range(CHUNKS):
        at = slice(r * step, (r + 1) * step)
        for i, to in enumerate(peer_ids):
            remote(part.at[i, at], part_in.at[i, at], part_s.at[i, r], part_r.at[i, r], to).wait_recv()
        value = total[at, :]
        for i in range(NX - 1):
            value = value + part_in[i, at, :].astype(F32)
        out_ref[at, :] = value.astype(BF16)
    for copy in sent:
        copy.wait_send()


def per_device(seq_size, x_in, gate_in, b_in, c_in, log_decay, w_out):
    rows, columns = x_in.shape
    states = b_in.shape[1]
    depth = NY * NC * columns
    dma = pltpu.SemaphoreType.DMA
    vmem = pl.BlockSpec(memory_space=pltpu.VMEM)
    return pl.pallas_call(
        functools.partial(kernel, seq_size),
        out_shape=jax.ShapeDtypeStruct((rows, columns), BF16),
        in_specs=[vmem] * 5 + [pl.BlockSpec(memory_space=pl.ANY)],
        out_specs=vmem,
        scratch_shapes=[
            pltpu.VMEM((SPAN, states + 16, columns), BF16),
            pltpu.VMEM((states + 16, columns), BF16),
            pltpu.VMEM((2, states + 16, columns), BF16),
            pltpu.VMEM((rows, columns), F32),
            pltpu.VMEM((rows, columns), F32),
            pltpu.VMEM((NY * NC, rows, columns), BF16),
            pltpu.VMEM((NX, depth, columns), BF16),
            pltpu.VMEM((rows, columns), F32),
            pltpu.VMEM((NX - 1, rows, columns), BF16),
            pltpu.VMEM((NX - 1, rows, columns), BF16),
            dma((SPAN - 1,)),
            dma((SPAN - 1,)),
            dma((2,)),
            dma((2,)),
            dma((NX - 1,)),
            dma((NX - 1,)),
            dma(()),
            dma((CHUNKS, 2, NY // 2)),
            dma((CHUNKS, 2, NY // 2)),
            dma((CHUNKS, NY)),
            dma((CHUNKS, NY)),
            dma((NX - 1, CHUNKS)),
            dma((NX - 1, CHUNKS)),
        ],
        compiler_params=pltpu.CompilerParams(
            collective_id=0, has_side_effects=True, vmem_limit_bytes=40 * 2**20
        ),
        name="ssd_layer",
    )(x_in, gate_in, b_in, c_in, log_decay, w_out)


def solution(mesh):
    in_specs = (
        P("seq", "head"),
        P("seq", "head"),
        P("seq", None),
        P("seq", None),
        P("head", "seq"),
        P(None, "head"),
    )
    return jax.shard_map(
        functools.partial(per_device, mesh.shape["seq"]),
        mesh=mesh,
        in_specs=in_specs,
        out_specs=P("seq", "head"),
        check_vma=False,
    )
```

```python
import functools

import jax
import jax.numpy as jnp
from jax import lax
from jax.experimental import pallas as pl
from jax.experimental.pallas import tpu as pltpu
from jax.sharding import PartitionSpec as P

MESH = pl.DeviceIdType.MESH
BLOCK = 256
NX, NY, NC = 4, 8, 2
SPAN = 4
CHUNKS = 4
NT = (((1,), (1,)), ((), ()))
TN = (((0,), (0,)), ((), ()))
F32 = jnp.float32
BF16 = jnp.bfloat16


def exact(a, b):
    return lax.dot_general(a, b, NT, precision=lax.Precision.HIGHEST, preferred_element_type=F32)


def pack(ref, state, total):
    n = state.shape[0]
    row = lax.broadcasted_iota(jnp.int32, (16, state.shape[1]), 0)
    high = total.astype(BF16).astype(F32)
    tail = jnp.where(row == 0, high, jnp.where(row == 1, total - high, 0.0))
    ref[0:n, :] = state.astype(BF16)
    ref[n : n + 16, :] = tail.astype(BF16)


def unpack(ref, n):
    tail = ref[n : n + 16, :].astype(F32)
    return ref[0:n, :].astype(F32), tail[0:1] + tail[1:2]


def kernel(
    seq_size,
    x_hbm,
    gate_hbm,
    b_hbm,
    c_hbm,
    decay_hbm,
    w_ref,
    out_ref,
    x_ref,
    gate_ref,
    b_ref,
    c_ref,
    decay_ref,
    m1,
    m2,
    m2_in,
    start_ref,
    diag,
    wide,
    blocks,
    w_buf,
    total,
    part,
    part_in,
    m1_s,
    m1_r,
    m2_s,
    m2_r,
    ready,
    w_s,
    w_r,
    own_s,
    in_s,
    ring_s,
    ring_r,
    twin_s,
    twin_r,
    part_s,
    part_r,
):
    rows, columns = x_ref.shape
    states = b_ref.shape[1]
    channels = columns // decay_ref.shape[0]
    step = rows // CHUNKS
    s = lax.axis_index("seq")
    head = lax.axis_index("head")
    px, py, core = head // (NY * NC), (head // NC) % NY, head % NC
    group, place = s // SPAN, s % SPAN
    groups = seq_size // SPAN

    def device(z, x, y, c):
        return (z, (x * NY + y) * NC + c)

    mates = [(place + i) % SPAN for i in range(1, SPAN)]
    mate_ids = [device(group * SPAN + m, px, py, core) for m in mates]
    ahead_ids = [device((s + SPAN * i) % seq_size, px, py, core) for i in (1, 2)]
    behind_ids = [device((s + seq_size - SPAN * i) % seq_size, px, py, core) for i in (1, 2)]
    peers = [(px + i) % NX for i in range(1, NX)]
    peer_ids = [device(s, p, py, core) for p in peers]
    up = device(s, px, (py + 1) % NY, core)
    down = device(s, px, (py + NY - 1) % NY, core)
    twin = device(s, px, py, 1 - core)

    def remote(src, dst, send, recv, to):
        return pltpu.make_async_remote_copy(
            src_ref=src, dst_ref=dst, send_sem=send, recv_sem=recv, device_id=to, device_id_type=MESH
        )

    loads = [
        pltpu.make_async_copy(src, dst, in_s.at[i])
        for i, (src, dst) in enumerate(
            (
                (decay_hbm, decay_ref),
                (b_hbm, b_ref),
                (x_hbm, x_ref),
                (c_hbm, c_ref),
                (gate_hbm, gate_ref),
            )
        )
    ]
    for load in loads:
        load.start()

    partners = mate_ids + peer_ids + [up, down, twin]
    barrier = pltpu.get_barrier_semaphore()

    def signal(sem, to):
        pl.semaphore_signal(sem, inc=1, device_id=to, device_id_type=MESH)

    for to in partners:
        signal(barrier, to)
    for i, to in enumerate(ahead_ids):

        @pl.when(group + i + 1 < groups)
        def _():
            signal(barrier, to)

    depth = NY * NC * columns
    own_w = pltpu.make_async_copy(w_ref.at[pl.ds(px * depth, depth), :], w_buf.at[px], own_s)
    own_w.start()
    t_of = lax.broadcasted_iota(jnp.int32, (BLOCK, BLOCK), 0)
    s_of = lax.broadcasted_iota(jnp.int32, (BLOCK, BLOCK), 1)
    lower = s_of <= t_of
    ones = jnp.where(lower, 1.0, 0.0)
    first_head = lax.broadcasted_iota(jnp.int32, (BLOCK, columns), 1) < channels
    first_row = lax.broadcasted_iota(jnp.int32, (columns, BLOCK), 0) < channels
    local, cum_last = [], []
    for load in loads[:3]:
        load.wait()
    for q in range(rows // BLOCK):
        at = slice(q * BLOCK, (q + 1) * BLOCK)
        decay = decay_ref[:, at]
        cum = exact(ones, jnp.where(first_row, decay[0:1], decay[1:2]))
        wide[at, :] = cum
        last = cum[BLOCK - 1 :, :]
        to_end = jnp.exp(last - cum)
        b = b_ref[at, :].astype(F32)
        x = x_ref[at, :]
        halves = [
            lax.dot_general(
                (b * to_end[:, h * channels : h * channels + 1]).astype(BF16),
                x,
                TN,
                preferred_element_type=F32,
            )
            for h in range(2)
        ]
        local.append(jnp.where(first_head[:states], halves[0], halves[1]))
        cum_last.append(last)
    m1_own = m1.at[place]
    pack(
        m1_own,
        local[0] * jnp.exp(cum_last[1]) + local[1],
        jnp.exp(cum_last[0] + cum_last[1]),
    )

    pl.semaphore_wait(barrier, len(partners) + group)
    sent = []
    for i, to in enumerate(mate_ids):
        copy = remote(m1_own, m1_own, m1_s.at[i], m1_r.at[i], to)

        @pl.when((group < groups - 1) | (place + i + 1 < SPAN))
        def _():
            copy.start()

    for i, to in enumerate(behind_ids):

        @pl.when(group >= i + 1)
        def _():
            signal(ready.at[i], to)

    for i, to in enumerate(peer_ids):
        copy = remote(
            w_ref.at[pl.ds(peers[i] * depth, depth), :], w_buf.at[px], w_s.at[i], w_r.at[i], to
        )
        copy.start()
        sent.append(copy)

    for load in loads[3:]:
        load.wait()
    for q in range(rows // BLOCK):
        at = slice(q * BLOCK, (q + 1) * BLOCK)
        decay = decay_ref[:, at]
        cum = wide[at, :]
        x = x_ref[at, :]
        scores = lax.dot_general(c_ref[at, :], b_ref[at, :], NT, preferred_element_type=F32)
        along = exact(jnp.where(first_row[56:72], decay[0:1], decay[1:2]), ones)
        halves = []
        for h in range(2):
            gap = cum[:, h * channels : h * channels + 1] - along[8 * h : 8 * h + 1, :]
            weights = jnp.where(lower, scores * jnp.exp(jnp.where(lower, gap, 0.0)), 0.0)
            halves.append(jnp.dot(weights.astype(BF16), x, preferred_element_type=F32))
        diag[at, :] = jnp.where(first_head, halves[0], halves[1])

    for i in range(SPAN - 1):
        slot = m1.at[(place + SPAN - 1 - i) % SPAN]

        @pl.when((group < groups - 1) | (place >= i + 1))
        def _():
            remote(slot, slot, m1_s.at[i], m1_r.at[i], mate_ids[i]).wait_recv()

    state = jnp.zeros((states, columns), F32)
    decayed = jnp.ones((1, columns), F32)
    before, before_decay = state, decayed
    for i in range(SPAN):
        before = jnp.where(place == i, state, before)
        before_decay = jnp.where(place == i, decayed, before_decay)
        more, its_decay = unpack(m1.at[i], states)
        state = state * its_decay + more
        decayed = decayed * its_decay

    @pl.when(group < groups - 1)
    def _():
        pack(m2, state, decayed)

    for i, to in enumerate(ahead_ids):

        @pl.when(group + i + 1 < groups)
        def _():
            pl.semaphore_wait(ready.at[i], 1)
            remote(m2, m2_in.at[i], m2_s.at[i], m2_r.at[i], to).start()

    start_ref[...] = before

    @pl.when(group == 1)
    def _():
        remote(m2, m2_in.at[0], m2_s.at[0], m2_r.at[0], ahead_ids[0]).wait_recv()
        near, _ = unpack(m2_in.at[0], states)
        start_ref[...] = before + near * before_decay

    @pl.when(group == 2)
    def _():
        for i, to in enumerate(ahead_ids):
            remote(m2, m2_in.at[i], m2_s.at[i], m2_r.at[i], to).wait_recv()
        near, near_decay = unpack(m2_in.at[0], states)
        far, _ = unpack(m2_in.at[1], states)
        start_ref[...] = before + (far * near_decay + near) * before_decay

    start = start_ref[...]
    starts = [start, start * jnp.exp(cum_last[0]) + local[0]]

    mine = py * NC + core
    for r in range(CHUNKS):
        at = slice(r * step, (r + 1) * step)
        start_bf = starts[r * step // BLOCK].astype(BF16)
        carry = jnp.dot(c_ref[at, :], start_bf, preferred_element_type=F32)
        y = diag[at, :] + carry * jnp.exp(wide[at, :])
        gate = gate_ref[at, :].astype(F32)
        blocks[mine, at, :] = (y * (gate / (1.0 + jnp.exp(-gate)))).astype(BF16)
        here = blocks.at[mine, at]
        for d, to in enumerate((up, down)):
            copy = remote(here, here, ring_s.at[r, d, 0], ring_r.at[r, d, 0], to)
            copy.start()
            sent.append(copy)
        copy = remote(here, here, twin_s.at[r, 0], twin_r.at[r, 0], twin)
        copy.start()
        sent.append(copy)

    def hops(r, d):
        return NY // 2 if (r + d) % 2 == 0 else NY // 2 - 1

    def behind(hop, d):
        return (py + NY - hop) % NY if d == 0 else (py + hop) % NY

    for hop in range(1, NY // 2 + 1):
        for r in range(CHUNKS):
            at = slice(r * step, (r + 1) * step)
            for d, to in enumerate((up, down)):
                if hop > hops(r, d):
                    continue
                here = blocks.at[behind(hop, d) * NC + core, at]
                remote(here, here, ring_s.at[r, d, hop - 1], ring_r.at[r, d, hop - 1], to).wait_recv()
                if hop < hops(r, d):
                    copy = remote(here, here, ring_s.at[r, d, hop], ring_r.at[r, d, hop], to)
                    copy.start()
                    sent.append(copy)
                which = 2 * hop - 1 + d if hop < NY // 2 else NY - 1
                copy = remote(here, here, twin_s.at[r, which], twin_r.at[r, which], twin)
                copy.start()
                sent.append(copy)

    own_w.wait()
    for i in range(NX - 1):
        slot = w_buf.at[(px + NX - 1 - i) % NX]
        remote(slot, slot, w_s.at[i], w_r.at[i], peer_ids[i]).wait_recv()
    for r in range(CHUNKS):
        at = slice(r * step, (r + 1) * step)
        for which in range(NY):
            if which == 0:
                where = py
            elif which < NY - 1:
                where = behind((which + 1) // 2, (which + 1) % 2)
            else:
                where = (py + NY // 2) % NY
            there = blocks.at[where * NC + 1 - core, at]
            remote(there, there, twin_s.at[r, which], twin_r.at[r, which], twin).wait_recv()
        gathered = jnp.concatenate([blocks[k, at, :] for k in range(NY * NC)], axis=1)
        for i, to in enumerate(peer_ids):
            part[i, at, :] = jnp.dot(
                gathered, w_buf[peers[i]], preferred_element_type=F32
            ).astype(BF16)
            copy = remote(part.at[i, at], part_in.at[i, at], part_s.at[i, r], part_r.at[i, r], to)
            copy.start()
            sent.append(copy)
        total[at, :] = jnp.dot(gathered, w_buf[px], preferred_element_type=F32)
    for r in range(CHUNKS):
        at = slice(r * step, (r + 1) * step)
        for i, to in enumerate(peer_ids):
            remote(part.at[i, at], part_in.at[i, at], part_s.at[i, r], part_r.at[i, r], to).wait_recv()
        value = total[at, :]
        for i in range(NX - 1):
            value = value + part_in[i, at, :].astype(F32)
        out_ref[at, :] = value.astype(BF16)
    for copy in sent:
        copy.wait_send()
    for i, to in enumerate(mate_ids):

        @pl.when((group < groups - 1) | (place + i + 1 < SPAN))
        def _():
            remote(m1_own, m1_own, m1_s.at[i], m1_r.at[i], to).wait_send()

    for i, to in enumerate(ahead_ids):

        @pl.when(group + i + 1 < groups)
        def _():
            remote(m2, m2_in.at[i], m2_s.at[i], m2_r.at[i], to).wait_send()


def per_device(seq_size, x_in, gate_in, b_in, c_in, log_decay, w_out):
    rows, columns = x_in.shape
    states = b_in.shape[1]
    depth = NY * NC * columns
    dma = pltpu.SemaphoreType.DMA
    vmem = pl.BlockSpec(memory_space=pltpu.VMEM)
    return pl.pallas_call(
        functools.partial(kernel, seq_size),
        out_shape=pltpu.VMEM((rows, columns), BF16),
        in_specs=[pl.BlockSpec(memory_space=pltpu.HBM)] * 6,
        out_specs=vmem,
        scratch_shapes=[
            pltpu.VMEM((rows, columns), BF16),
            pltpu.VMEM((rows, columns), BF16),
            pltpu.VMEM((rows, states), BF16),
            pltpu.VMEM((rows, states), BF16),
            pltpu.VMEM(log_decay.shape, F32),
            pltpu.VMEM((SPAN, states + 16, columns), BF16),
            pltpu.VMEM((states + 16, columns), BF16),
            pltpu.VMEM((2, states + 16, columns), BF16),
            pltpu.VMEM((states, columns), F32),
            pltpu.VMEM((rows, columns), F32),
            pltpu.VMEM((rows, columns), F32),
            pltpu.VMEM((NY * NC, rows, columns), BF16),
            pltpu.VMEM((NX, depth, columns), BF16),
            pltpu.VMEM((rows, columns), F32),
            pltpu.VMEM((NX - 1, rows, columns), BF16),
            pltpu.VMEM((NX - 1, rows, columns), BF16),
            dma((SPAN - 1,)),
            dma((SPAN - 1,)),
            dma((2,)),
            dma((2,)),
            pltpu.SemaphoreType.REGULAR((2,)),
            dma((NX - 1,)),
            dma((NX - 1,)),
            dma(()),
            dma((5,)),
            dma((CHUNKS, 2, NY // 2)),
            dma((CHUNKS, 2, NY // 2)),
            dma((CHUNKS, NY)),
            dma((CHUNKS, NY)),
            dma((NX - 1, CHUNKS)),
            dma((NX - 1, CHUNKS)),
        ],
        compiler_params=pltpu.CompilerParams(
            collective_id=0, has_side_effects=True, vmem_limit_bytes=56 * 2**20
        ),
        name="ssd_layer",
    )(x_in, gate_in, b_in, c_in, log_decay, w_out)


def solution(mesh):
    in_specs = (
        P("seq", "head"),
        P("seq", "head"),
        P("seq", None),
        P("seq", None),
        P("head", "seq"),
        P(None, "head"),
    )
    return jax.shard_map(
        functools.partial(per_device, mesh.shape["seq"]),
        mesh=mesh,
        in_specs=in_specs,
        out_specs=P("seq", "head"),
        check_vma=False,
    )
```

```python
import functools

import jax
import jax.numpy as jnp
from jax import lax
from jax.experimental import pallas as pl
from jax.experimental.pallas import tpu as pltpu
from jax.sharding import PartitionSpec as P

MESH = pl.DeviceIdType.MESH
BLOCK = 256
NX, NY, NC = 4, 8, 2
SPAN = 4
CHUNKS = 4
NT = (((1,), (1,)), ((), ()))
TN = (((0,), (0,)), ((), ()))
F32 = jnp.float32
BF16 = jnp.bfloat16


def exact(a, b):
    return lax.dot_general(a, b, NT, precision=lax.Precision.HIGHEST, preferred_element_type=F32)


def pack(ref, state, total):
    n = state.shape[0]
    row = lax.broadcasted_iota(jnp.int32, (16, state.shape[1]), 0)
    high = total.astype(BF16).astype(F32)
    tail = jnp.where(row == 0, high, jnp.where(row == 1, total - high, 0.0))
    ref[0:n, :] = state.astype(BF16)
    ref[n : n + 16, :] = tail.astype(BF16)


def unpack(ref, n):
    tail = ref[n : n + 16, :].astype(F32)
    return ref[0:n, :].astype(F32), tail[0:1] + tail[1:2]


def kernel(
    seq_size,
    x_hbm,
    gate_hbm,
    b_hbm,
    c_hbm,
    decay_hbm,
    w_ref,
    out_ref,
    x_ref,
    gate_ref,
    b_ref,
    c_ref,
    decay_ref,
    own_state,
    m2,
    state_in,
    start_ref,
    diag,
    wide,
    blocks,
    w_buf,
    total,
    part,
    part_in,
    m1_s,
    m1_r,
    m2_s,
    m2_r,
    ready,
    w_s,
    w_r,
    swap_s,
    swap_r,
    own_s,
    in_s,
    ring_s,
    ring_r,
    twin_s,
    twin_r,
    part_s,
    part_r,
):
    rows, columns = x_ref.shape
    states = b_ref.shape[1]
    channels = columns // decay_ref.shape[0]
    step = rows // CHUNKS
    s = lax.axis_index("seq")
    head = lax.axis_index("head")
    px, py, core = head // (NY * NC), (head // NC) % NY, head % NC
    group, place, odd = s // SPAN, s % SPAN, s % 2
    groups = seq_size // SPAN
    opening = group == 0

    def device(z, x, y, c):
        return (z, (x * NY + y) * NC + c)

    mate = device(s + 1 - 2 * odd, px, py, core)
    def after(i):
        return device((s + i) % seq_size, px, py, core)

    mates = [device(group * SPAN + (place + i) % SPAN, px, py, core) for i in range(1, SPAN)]
    to_mates = [opening | (odd == 0) if i == 0 else opening for i in range(SPAN - 1)]
    from_mates = [opening | (odd == 1) if i == 0 else opening for i in range(SPAN - 1)]
    pair_end = (group > 0) & (place == 1)
    group_end = (group == 1) & (place == SPAN - 1)
    late_pair, late, closing = (group > 0) & (place >= 2), group > 0, group == groups - 1
    pair_from = device(group * SPAN + 1, px, py, core)
    group_from = device(2 * SPAN - 1, px, py, core)
    opening_from = device(place, px, py, core)
    peers = [(px + i) % NX for i in range(1, NX)]
    peer_ids = [device(s, p, py, core) for p in peers]
    up = device(s, px, (py + 1) % NY, core)
    down = device(s, px, (py + NY - 1) % NY, core)
    twin = device(s, px, py, 1 - core)

    def remote(src, dst, send, recv, to):
        return pltpu.make_async_remote_copy(
            src_ref=src, dst_ref=dst, send_sem=send, recv_sem=recv, device_id=to, device_id_type=MESH
        )

    loads = [
        pltpu.make_async_copy(src, dst, in_s.at[i])
        for i, (src, dst) in enumerate(
            (
                (decay_hbm, decay_ref),
                (b_hbm, b_ref),
                (x_hbm, x_ref),
                (c_hbm, c_ref),
                (gate_hbm, gate_ref),
            )
        )
    ]
    for load in loads:
        load.start()

    partners = peer_ids + [up, down, twin]
    barrier = pltpu.get_barrier_semaphore()

    def signal(sem, to):
        pl.semaphore_signal(sem, inc=1, device_id=to, device_id_type=MESH)

    for to in partners:
        signal(barrier, to)
    sends = [(opening, after(SPAN * i), i - 1, 2) for i in (1, 2)]
    sends += [(pair_end, after(i), i - 1, 0) for i in (1, 2)]
    sends += [(group_end, after(i), i - 1, 1) for i in (1, 2, 3, 4)]
    for use, to, _, _ in sends:

        @pl.when(use)
        def _():
            signal(barrier, to)

    @pl.when(opening)
    def _():
        for i in range(1, SPAN):
            signal(barrier, mates[i - 1])

    @pl.when(late)
    def _():
        signal(barrier, mate)

    greetings = jnp.where(opening, SPAN - 1, 2 + place // 2 + group // 2)
    pl.semaphore_wait(barrier, len(partners) + greetings)

    @pl.when(late)
    def _():
        signal(ready.at[group - 1], opening_from)

    @pl.when(late_pair)
    def _():
        signal(ready.at[place - 2], pair_from)

    @pl.when(closing)
    def _():
        signal(ready.at[place], group_from)

    sent = []
    depth = NY * NC * columns
    half = depth // 2
    for i in (1, 0, 2):
        at, n = (odd * half, half) if i == 1 else (0, depth)
        copy = remote(
            w_ref.at[pl.ds(peers[i] * depth + at, n), :],
            w_buf.at[px, pl.ds(at, n)],
            w_s.at[i],
            w_r.at[i],
            peer_ids[i],
        )
        copy.start()
        sent.append(copy)
    opposite = (px + NX // 2) % NX

    def swap(mine):
        slot = w_buf.at[opposite, pl.ds((odd if mine else 1 - odd) * half, half)]
        return slot, remote(slot, slot, swap_s, swap_r, mate)

    def start_swap():
        slot, copy = swap(True)
        remote(slot, slot, w_s.at[1], w_r.at[1], peer_ids[1]).wait_recv()
        copy.start()

    own_w = pltpu.make_async_copy(w_ref.at[pl.ds(px * depth, depth), :], w_buf.at[px], own_s)
    own_w.start()
    t_of = lax.broadcasted_iota(jnp.int32, (BLOCK, BLOCK), 0)
    s_of = lax.broadcasted_iota(jnp.int32, (BLOCK, BLOCK), 1)
    lower = s_of <= t_of
    ones = jnp.where(lower, 1.0, 0.0)
    first_head = lax.broadcasted_iota(jnp.int32, (BLOCK, columns), 1) < channels
    first_row = lax.broadcasted_iota(jnp.int32, (columns, BLOCK), 0) < channels
    local, cum_last = [], []
    for load in loads[:3]:
        load.wait()
    for q in range(rows // BLOCK):
        at = slice(q * BLOCK, (q + 1) * BLOCK)
        decay = decay_ref[:, at]
        cum = exact(ones, jnp.where(first_row, decay[0:1], decay[1:2]))
        wide[at, :] = cum
        last = cum[BLOCK - 1 :, :]
        to_end = jnp.exp(last - cum)
        b = b_ref[at, :].astype(F32)
        x = x_ref[at, :]
        halves = [
            lax.dot_general(
                (b * to_end[:, h * channels : h * channels + 1]).astype(BF16),
                x,
                TN,
                preferred_element_type=F32,
            )
            for h in range(2)
        ]
        local.append(jnp.where(first_head[:states], halves[0], halves[1]))
        cum_last.append(last)
    pack(
        own_state.at[place],
        local[0] * jnp.exp(cum_last[1]) + local[1],
        jnp.exp(cum_last[0] + cum_last[1]),
    )

    def to_mate(i):
        slot = own_state.at[place]
        return remote(slot, slot, m1_s.at[i], m1_r.at[i], mates[i])

    for i in range(SPAN - 1):

        @pl.when(to_mates[i])
        def _():
            to_mate(i).start()

    for load in loads[3:]:
        load.wait()
    for q in range(rows // BLOCK):
        at = slice(q * BLOCK, (q + 1) * BLOCK)
        decay = decay_ref[:, at]
        cum = wide[at, :]
        x = x_ref[at, :]
        scores = lax.dot_general(c_ref[at, :], b_ref[at, :], NT, preferred_element_type=F32)
        along = exact(jnp.where(first_row[56:72], decay[0:1], decay[1:2]), ones)
        halves = []
        for h in range(2):
            gap = cum[:, h * channels : h * channels + 1] - along[8 * h : 8 * h + 1, :]
            weights = jnp.where(lower, scores * jnp.exp(jnp.where(lower, gap, 0.0)), 0.0)
            halves.append(jnp.dot(weights.astype(BF16), x, preferred_element_type=F32))
        diag[at, :] = jnp.where(first_head, halves[0], halves[1])

    def send(chosen):
        for use, to, i, k in chosen:

            @pl.when(use)
            def _():
                pl.semaphore_wait(ready.at[i], 1)
                remote(m2, state_in.at[k], m2_s.at[i], m2_r.at[k], to).start()

    def state_from(k):
        remote(m2, state_in.at[k], m2_s.at[0], m2_r.at[k], mate).wait_recv()
        return unpack(state_in.at[k], states)

    for i in range(SPAN - 1):

        @pl.when(from_mates[i])
        def _():
            slot = own_state.at[(place + SPAN - 1 - i) % SPAN]
            remote(slot, slot, m1_s.at[i], m1_r.at[i], mates[i]).wait_recv()

    @pl.when(opening)
    def _():
        state = jnp.zeros((states, columns), F32)
        before = state
        decay = jnp.ones((1, columns), F32)
        for i in range(SPAN):
            before = jnp.where(place == i, state, before)
            more, its_decay = unpack(own_state.at[i], states)
            state = state * its_decay + more
            decay = decay * its_decay
        pack(m2, state, decay)
        start_ref[...] = before

    send(sends[:1])

    def joined():
        state, decay = unpack(own_state.at[place], states)
        more, its_decay = unpack(own_state.at[jnp.maximum(place - 1, 0)], states)
        return more * decay + state, decay * its_decay

    @pl.when(pair_end)
    def _():
        pack(m2, *joined())

    send(sends[2:4])

    @pl.when(group_end)
    def _():
        state, decay = joined()
        more, its_decay = state_from(0)
        pack(m2, more * decay + state, decay * its_decay)

    send(sends[4:])

    @pl.when(late)
    def _():
        start_ref[...] = state_from(2)[0]

    @pl.when(closing)
    def _():
        more, its_decay = state_from(1)
        start_ref[...] = start_ref[...] * its_decay + more

    @pl.when(late_pair & jnp.logical_not(group_end))
    def _():
        state_from(0)

    @pl.when(late_pair)
    def _():
        more, its_decay = unpack(state_in.at[0], states)
        start_ref[...] = start_ref[...] * its_decay + more

    @pl.when(late & (odd == 1))
    def _():
        more, its_decay = unpack(own_state.at[jnp.maximum(place - 1, 0)], states)
        start_ref[...] = start_ref[...] * its_decay + more

    start = start_ref[...]
    starts = [start, start * jnp.exp(cum_last[0]) + local[0]]

    mine = py * NC + core
    for r in range(CHUNKS):
        at = slice(r * step, (r + 1) * step)
        start_bf = starts[r * step // BLOCK].astype(BF16)
        carry = jnp.dot(c_ref[at, :], start_bf, preferred_element_type=F32)
        y = diag[at, :] + carry * jnp.exp(wide[at, :])
        gate = gate_ref[at, :].astype(F32)
        blocks[mine, at, :] = (y * (gate / (1.0 + jnp.exp(-gate)))).astype(BF16)
        here = blocks.at[mine, at]
        for d, to in enumerate((up, down)):
            copy = remote(here, here, ring_s.at[r, d, 0], ring_r.at[r, d, 0], to)
            copy.start()
            sent.append(copy)
        copy = remote(here, here, twin_s.at[r, 0], twin_r.at[r, 0], twin)
        copy.start()
        sent.append(copy)

    send(sends[1:2])

    @pl.when(group > 0)
    def _():
        start_swap()

    def hops(r, d):
        return NY // 2 if (r + d) % 2 == 0 else NY // 2 - 1

    def behind(hop, d):
        return (py + NY - hop) % NY if d == 0 else (py + hop) % NY

    for hop in range(1, NY // 2 + 1):
        if hop == 2:

            @pl.when(group == 0)
            def _():
                start_swap()

        for r in range(CHUNKS):
            at = slice(r * step, (r + 1) * step)
            for d, to in enumerate((up, down)):
                if hop > hops(r, d):
                    continue
                here = blocks.at[behind(hop, d) * NC + core, at]
                remote(here, here, ring_s.at[r, d, hop - 1], ring_r.at[r, d, hop - 1], to).wait_recv()
                if hop < hops(r, d):
                    copy = remote(here, here, ring_s.at[r, d, hop], ring_r.at[r, d, hop], to)
                    copy.start()
                    sent.append(copy)
                which = 2 * hop - 1 + d if hop < NY // 2 else NY - 1
                copy = remote(here, here, twin_s.at[r, which], twin_r.at[r, which], twin)
                copy.start()
                sent.append(copy)

    own_w.wait()
    for i in (0, 2):
        slot = w_buf.at[(px + NX - 1 - i) % NX]
        remote(slot, slot, w_s.at[i], w_r.at[i], peer_ids[i]).wait_recv()
    swap(False)[1].wait_recv()
    for r in range(CHUNKS):
        at = slice(r * step, (r + 1) * step)
        for which in range(NY):
            if which == 0:
                where = py
            elif which < NY - 1:
                where = behind((which + 1) // 2, (which + 1) % 2)
            else:
                where = (py + NY // 2) % NY
            there = blocks.at[where * NC + 1 - core, at]
            remote(there, there, twin_s.at[r, which], twin_r.at[r, which], twin).wait_recv()
        gathered = jnp.concatenate([blocks[k, at, :] for k in range(NY * NC)], axis=1)
        for i, to in enumerate(peer_ids):
            part[i, at, :] = jnp.dot(
                gathered, w_buf[peers[i]], preferred_element_type=F32
            ).astype(BF16)
            copy = remote(part.at[i, at], part_in.at[i, at], part_s.at[i, r], part_r.at[i, r], to)
            copy.start()
            sent.append(copy)
        total[at, :] = jnp.dot(gathered, w_buf[px], preferred_element_type=F32)
    for r in range(CHUNKS):
        at = slice(r * step, (r + 1) * step)
        for i, to in enumerate(peer_ids):
            remote(part.at[i, at], part_in.at[i, at], part_s.at[i, r], part_r.at[i, r], to).wait_recv()
        value = total[at, :]
        for i in range(NX - 1):
            value = value + part_in[i, at, :].astype(F32)
        out_ref[at, :] = value.astype(BF16)
    for copy in sent:
        copy.wait_send()

    for i in range(SPAN - 1):

        @pl.when(to_mates[i])
        def _():
            to_mate(i).wait_send()

    swap(True)[1].wait_send()
    for use, to, i, k in sends:

        @pl.when(use)
        def _():
            remote(m2, state_in.at[k], m2_s.at[i], m2_r.at[k], to).wait_send()


def per_device(seq_size, x_in, gate_in, b_in, c_in, log_decay, w_out):
    rows, columns = x_in.shape
    states = b_in.shape[1]
    depth = NY * NC * columns
    dma = pltpu.SemaphoreType.DMA
    vmem = pl.BlockSpec(memory_space=pltpu.VMEM)
    return pl.pallas_call(
        functools.partial(kernel, seq_size),
        out_shape=pltpu.VMEM((rows, columns), BF16),
        in_specs=[pl.BlockSpec(memory_space=pltpu.HBM)] * 6,
        out_specs=vmem,
        scratch_shapes=[
            pltpu.VMEM((rows, columns), BF16),
            pltpu.VMEM((rows, columns), BF16),
            pltpu.VMEM((rows, states), BF16),
            pltpu.VMEM((rows, states), BF16),
            pltpu.VMEM(log_decay.shape, F32),
            pltpu.VMEM((SPAN, states + 16, columns), BF16),
            pltpu.VMEM((states + 16, columns), BF16),
            pltpu.VMEM((3, states + 16, columns), BF16),
            pltpu.VMEM((states, columns), F32),
            pltpu.VMEM((rows, columns), F32),
            pltpu.VMEM((rows, columns), F32),
            pltpu.VMEM((NY * NC, rows, columns), BF16),
            pltpu.VMEM((NX, depth, columns), BF16),
            pltpu.VMEM((rows, columns), F32),
            pltpu.VMEM((NX - 1, rows, columns), BF16),
            pltpu.VMEM((NX - 1, rows, columns), BF16),
            dma((SPAN - 1,)),
            dma((SPAN - 1,)),
            dma((SPAN,)),
            dma((3,)),
            pltpu.SemaphoreType.REGULAR((SPAN,)),
            dma((NX - 1,)),
            dma((NX - 1,)),
            dma(()),
            dma(()),
            dma(()),
            dma((5,)),
            dma((CHUNKS, 2, NY // 2)),
            dma((CHUNKS, 2, NY // 2)),
            dma((CHUNKS, NY)),
            dma((CHUNKS, NY)),
            dma((NX - 1, CHUNKS)),
            dma((NX - 1, CHUNKS)),
        ],
        compiler_params=pltpu.CompilerParams(
            collective_id=0, has_side_effects=True, vmem_limit_bytes=56 * 2**20
        ),
        name="ssd_layer",
    )(x_in, gate_in, b_in, c_in, log_decay, w_out)


def solution(mesh):
    in_specs = (
        P("seq", "head"),
        P("seq", "head"),
        P("seq", None),
        P("seq", None),
        P("head", "seq"),
        P(None, "head"),
    )
    return jax.shard_map(
        functools.partial(per_device, mesh.shape["seq"]),
        mesh=mesh,
        in_specs=in_specs,
        out_specs=P("seq", "head"),
        check_vma=False,
    )
```

```python
import functools

import jax
import jax.numpy as jnp
from jax import lax
from jax.experimental import pallas as pl
from jax.experimental.pallas import tpu as pltpu
from jax.sharding import PartitionSpec as P

MESH = pl.DeviceIdType.MESH
BLOCK = 256
NX, NY, NC = 4, 8, 2
SPAN = 4
CHUNKS = 4
NT = (((1,), (1,)), ((), ()))
TN = (((0,), (0,)), ((), ()))
F32 = jnp.float32
BF16 = jnp.bfloat16


def exact(a, b):
    return lax.dot_general(a, b, NT, precision=lax.Precision.HIGHEST, preferred_element_type=F32)


def pack(ref, state, total):
    n = state.shape[0]
    row = lax.broadcasted_iota(jnp.int32, (16, state.shape[1]), 0)
    high = total.astype(BF16).astype(F32)
    tail = jnp.where(row == 0, high, jnp.where(row == 1, total - high, 0.0))
    ref[0:n, :] = state.astype(BF16)
    ref[n : n + 16, :] = tail.astype(BF16)


def unpack(ref, n):
    tail = ref[n : n + 16, :].astype(F32)
    return ref[0:n, :].astype(F32), tail[0:1] + tail[1:2]


def kernel(
    seq_size,
    x_hbm,
    gate_hbm,
    b_hbm,
    c_hbm,
    decay_hbm,
    w_ref,
    out_ref,
    x_ref,
    gate_ref,
    b_ref,
    c_ref,
    decay_ref,
    own_state,
    m2,
    state_in,
    start_ref,
    diag,
    wide,
    blocks,
    w_buf,
    total,
    part,
    part_in,
    m1_s,
    m1_r,
    m2_s,
    m2_r,
    ready,
    w_s,
    w_r,
    swap_s,
    swap_r,
    own_s,
    in_s,
    ring_s,
    ring_r,
    twin_s,
    twin_r,
    part_s,
    part_r,
):
    rows, columns = x_ref.shape
    states = b_ref.shape[1]
    channels = columns // decay_ref.shape[0]
    step = rows // CHUNKS
    s = lax.axis_index("seq")
    head = lax.axis_index("head")
    px, py, core = head // (NY * NC), (head // NC) % NY, head % NC
    group, place, odd = s // SPAN, s % SPAN, s % 2
    groups = seq_size // SPAN
    opening = group == 0

    def device(z, x, y, c):
        return (z, (x * NY + y) * NC + c)

    mate = device(s + 1 - 2 * odd, px, py, core)
    def after(i):
        return device((s + i) % seq_size, px, py, core)

    mates = [device(group * SPAN + (place + i) % SPAN, px, py, core) for i in range(1, SPAN)]
    to_mates = [opening | (odd == 0) if i == 0 else opening for i in range(SPAN - 1)]
    from_mates = [
        (opening & (place >= i + 1)) | ((odd == 1) if i == 0 else False) for i in range(SPAN - 1)
    ]
    pair_end = (group > 0) & (place == 1)
    group_end = (group == 1) & (place == SPAN - 1)
    late_pair, late, closing = (group > 0) & (place >= 2), group > 0, group == groups - 1
    pair_from = device(group * SPAN + 1, px, py, core)
    group_from = device(2 * SPAN - 1, px, py, core)
    opening_from = device(place, px, py, core)
    peers = [(px + i) % NX for i in range(1, NX)]
    peer_ids = [device(s, p, py, core) for p in peers]
    up = device(s, px, (py + 1) % NY, core)
    down = device(s, px, (py + NY - 1) % NY, core)
    twin = device(s, px, py, 1 - core)

    def remote(src, dst, send, recv, to):
        return pltpu.make_async_remote_copy(
            src_ref=src, dst_ref=dst, send_sem=send, recv_sem=recv, device_id=to, device_id_type=MESH
        )

    loads = [
        pltpu.make_async_copy(src, dst, in_s.at[i])
        for i, (src, dst) in enumerate(
            (
                (decay_hbm, decay_ref),
                (b_hbm, b_ref),
                (x_hbm, x_ref),
                (c_hbm, c_ref),
                (gate_hbm, gate_ref),
            )
        )
    ]
    for load in loads:
        load.start()

    partners = peer_ids + [up, down, twin]
    barrier = pltpu.get_barrier_semaphore()

    def signal(sem, to):
        pl.semaphore_signal(sem, inc=1, device_id=to, device_id_type=MESH)

    for to in partners:
        signal(barrier, to)
    sends = [(opening, after(SPAN * i), i - 1, 2) for i in (1, 2)]
    sends += [(pair_end, after(i), i - 1, 0) for i in (1, 2)]
    sends += [(group_end, after(i), i - 1, 1) for i in (1, 2, 3, 4)]
    for use, to, _, _ in sends:

        @pl.when(use)
        def _():
            signal(barrier, to)

    @pl.when(opening)
    def _():
        for i in range(1, SPAN):
            signal(barrier, mates[i - 1])

    @pl.when(late)
    def _():
        signal(barrier, mate)

    greetings = jnp.where(opening, SPAN - 1, 2 + place // 2 + group // 2)
    sent = []
    depth = NY * NC * columns
    half = depth // 2
    opposite = (px + NX // 2) % NX

    def swap(mine):
        slot = w_buf.at[opposite, pl.ds((odd if mine else 1 - odd) * half, half)]
        return slot, remote(slot, slot, swap_s, swap_r, mate)

    def start_swap():
        slot, copy = swap(True)
        remote(slot, slot, w_s.at[1], w_r.at[1], peer_ids[1]).wait_recv()
        copy.start()

    own_w = pltpu.make_async_copy(w_ref.at[pl.ds(px * depth, depth), :], w_buf.at[px], own_s)
    own_w.start()
    t_of = lax.broadcasted_iota(jnp.int32, (BLOCK, BLOCK), 0)
    s_of = lax.broadcasted_iota(jnp.int32, (BLOCK, BLOCK), 1)
    lower = s_of <= t_of
    ones = jnp.where(lower, 1.0, 0.0)
    first_head = lax.broadcasted_iota(jnp.int32, (BLOCK, columns), 1) < channels
    first_row = lax.broadcasted_iota(jnp.int32, (columns, BLOCK), 0) < channels
    local, cum_last = [], []
    for load in loads[:3]:
        load.wait()
    for q in range(rows // BLOCK):
        if q == 1:
            pl.semaphore_wait(barrier, len(partners) + greetings)

            @pl.when(late)
            def _():
                signal(ready.at[group - 1], opening_from)

            @pl.when(late_pair)
            def _():
                signal(ready.at[place - 2], pair_from)

            @pl.when(closing)
            def _():
                signal(ready.at[place], group_from)

            for i in (1, 0, 2):
                at, n = (odd * half, half) if i == 1 else (0, depth)
                copy = remote(
                    w_ref.at[pl.ds(peers[i] * depth + at, n), :],
                    w_buf.at[px, pl.ds(at, n)],
                    w_s.at[i],
                    w_r.at[i],
                    peer_ids[i],
                )
                copy.start()
                sent.append(copy)
        at = slice(q * BLOCK, (q + 1) * BLOCK)
        decay = decay_ref[:, at]
        cum = exact(ones, jnp.where(first_row, decay[0:1], decay[1:2]))
        wide[at, :] = cum
        last = cum[BLOCK - 1 :, :]
        to_end = jnp.exp(last - cum)
        b = b_ref[at, :].astype(F32)
        x = x_ref[at, :]
        halves = [
            lax.dot_general(
                (b * to_end[:, h * channels : h * channels + 1]).astype(BF16),
                x,
                TN,
                preferred_element_type=F32,
            )
            for h in range(2)
        ]
        local.append(jnp.where(first_head[:states], halves[0], halves[1]))
        cum_last.append(last)
    pack(
        own_state.at[place],
        local[0] * jnp.exp(cum_last[1]) + local[1],
        jnp.exp(cum_last[0] + cum_last[1]),
    )

    def to_mate(i):
        slot = own_state.at[place]
        return remote(slot, slot, m1_s.at[i], m1_r.at[i], mates[i])

    for i in range(SPAN - 1):

        @pl.when(to_mates[i])
        def _():
            to_mate(i).start()

    for load in loads[3:]:
        load.wait()
    for q in range(rows // BLOCK):
        at = slice(q * BLOCK, (q + 1) * BLOCK)
        decay = decay_ref[:, at]
        cum = wide[at, :]
        x = x_ref[at, :]
        scores = lax.dot_general(c_ref[at, :], b_ref[at, :], NT, preferred_element_type=F32)
        along = exact(jnp.where(first_row[56:72], decay[0:1], decay[1:2]), ones)
        halves = []
        for h in range(2):
            gap = cum[:, h * channels : h * channels + 1] - along[8 * h : 8 * h + 1, :]
            weights = jnp.where(lower, scores * jnp.exp(jnp.where(lower, gap, 0.0)), 0.0)
            halves.append(jnp.dot(weights.astype(BF16), x, preferred_element_type=F32))
        gate = gate_ref[at, :].astype(F32)
        gate = gate / (1.0 + jnp.exp(-gate))
        diag[at, :] = jnp.where(first_head, halves[0], halves[1]) * gate
        wide[at, :] = jnp.exp(cum) * gate

    def send(chosen):
        for use, to, i, k in chosen:

            @pl.when(use)
            def _():
                pl.semaphore_wait(ready.at[i], 1)
                remote(m2, state_in.at[k], m2_s.at[i], m2_r.at[k], to).start()

    def state_from(k):
        remote(m2, state_in.at[k], m2_s.at[0], m2_r.at[k], mate).wait_recv()
        return unpack(state_in.at[k], states)

    def wait_mates(chosen):
        for i in range(SPAN - 1):

            @pl.when(chosen[i])
            def _():
                slot = own_state.at[(place + SPAN - 1 - i) % SPAN]
                remote(slot, slot, m1_s.at[i], m1_r.at[i], mates[i]).wait_recv()

    wait_mates(from_mates)

    @pl.when(opening)
    def _():
        start_ref[...] = jnp.zeros_like(start_ref)

    for i in range(SPAN - 1):

        @pl.when(opening & (place > i))
        def _():
            more, its_decay = unpack(own_state.at[i], states)
            start_ref[...] = start_ref[...] * its_decay + more

    def send_total(use):
        @pl.when(use)
        def _():
            state, decay = unpack(own_state.at[0], states)
            for i in range(1, SPAN):
                more, its_decay = unpack(own_state.at[i], states)
                state, decay = state * its_decay + more, decay * its_decay
            pack(m2, state, decay)

        send([(use, to, i, k) for _, to, i, k in sends[:1]])

    send_total(opening & (place == SPAN - 1))

    def joined():
        state, decay = unpack(own_state.at[place], states)
        more, its_decay = unpack(own_state.at[jnp.maximum(place - 1, 0)], states)
        return more * decay + state, decay * its_decay

    @pl.when(pair_end)
    def _():
        pack(m2, *joined())

    send(sends[2:4])

    @pl.when(group_end)
    def _():
        state, decay = joined()
        more, its_decay = state_from(0)
        pack(m2, more * decay + state, decay * its_decay)

    send(sends[4:])

    @pl.when(late)
    def _():
        start_ref[...] = state_from(2)[0]

    @pl.when(closing)
    def _():
        more, its_decay = state_from(1)
        start_ref[...] = start_ref[...] * its_decay + more

    @pl.when(late_pair & jnp.logical_not(group_end))
    def _():
        state_from(0)

    @pl.when(late_pair)
    def _():
        more, its_decay = unpack(state_in.at[0], states)
        start_ref[...] = start_ref[...] * its_decay + more

    @pl.when(late & (odd == 1))
    def _():
        more, its_decay = unpack(own_state.at[jnp.maximum(place - 1, 0)], states)
        start_ref[...] = start_ref[...] * its_decay + more

    start = start_ref[...]
    starts = [start, start * jnp.exp(cum_last[0]) + local[0]]

    mine = py * NC + core
    for r in range(CHUNKS):
        at = slice(r * step, (r + 1) * step)
        start_bf = starts[r * step // BLOCK].astype(BF16)
        carry = jnp.dot(c_ref[at, :], start_bf, preferred_element_type=F32)
        blocks[mine, at, :] = (diag[at, :] + carry * wide[at, :]).astype(BF16)
        here = blocks.at[mine, at]
        for d, to in enumerate((up, down)):
            copy = remote(here, here, ring_s.at[r, d, 0], ring_r.at[r, d, 0], to)
            copy.start()
            sent.append(copy)
        copy = remote(here, here, twin_s.at[r, 0], twin_r.at[r, 0], twin)
        copy.start()
        sent.append(copy)

    wait_mates([opening & (place < i + 1) for i in range(SPAN - 1)])
    send_total(opening & (place < SPAN - 1))
    send(sends[1:2])

    def hops(r, d):
        return NY // 2 if (r + d) % 2 == 0 else NY // 2 - 1

    def behind(hop, d):
        return (py + NY - hop) % NY if d == 0 else (py + hop) % NY

    for hop in range(1, NY // 2 + 1):
        if hop == 2:

            start_swap()

        for r in range(CHUNKS):
            at = slice(r * step, (r + 1) * step)
            for d, to in enumerate((up, down)):
                if hop > hops(r, d):
                    continue
                here = blocks.at[behind(hop, d) * NC + core, at]
                remote(here, here, ring_s.at[r, d, hop - 1], ring_r.at[r, d, hop - 1], to).wait_recv()
                if hop < hops(r, d):
                    copy = remote(here, here, ring_s.at[r, d, hop], ring_r.at[r, d, hop], to)
                    copy.start()
                    sent.append(copy)
                which = 2 * hop - 1 + d if hop < NY // 2 else NY - 1
                copy = remote(here, here, twin_s.at[r, which], twin_r.at[r, which], twin)
                copy.start()
                sent.append(copy)

    own_w.wait()
    for i in (0, 2):
        slot = w_buf.at[(px + NX - 1 - i) % NX]
        remote(slot, slot, w_s.at[i], w_r.at[i], peer_ids[i]).wait_recv()
    swap(False)[1].wait_recv()
    for r in range(CHUNKS):
        at = slice(r * step, (r + 1) * step)
        for which in range(NY):
            if which == 0:
                where = py
            elif which < NY - 1:
                where = behind((which + 1) // 2, (which + 1) % 2)
            else:
                where = (py + NY // 2) % NY
            there = blocks.at[where * NC + 1 - core, at]
            remote(there, there, twin_s.at[r, which], twin_r.at[r, which], twin).wait_recv()
        gathered = jnp.concatenate([blocks[k, at, :] for k in range(NY * NC)], axis=1)
        for pair in ((1, 0), (2, None)):
            ws = [w_buf[px if i is None else peers[i]] for i in pair]
            both = jnp.dot(gathered, jnp.concatenate(ws, axis=1), preferred_element_type=F32)
            for k, i in enumerate(pair):
                value = both[:, k * columns : (k + 1) * columns]
                if i is None:
                    total[at, :] = value
                    continue
                part[i, at, :] = value.astype(BF16)
                copy = remote(
                    part.at[i, at], part_in.at[i, at], part_s.at[i, r], part_r.at[i, r], peer_ids[i]
                )
                copy.start()
                sent.append(copy)
    for r in range(CHUNKS):
        at = slice(r * step, (r + 1) * step)
        for i, to in enumerate(peer_ids):
            remote(part.at[i, at], part_in.at[i, at], part_s.at[i, r], part_r.at[i, r], to).wait_recv()
        value = total[at, :]
        for i in range(NX - 1):
            value = value + part_in[i, at, :].astype(F32)
        out_ref[at, :] = value.astype(BF16)
    for copy in sent:
        copy.wait_send()

    for i in range(SPAN - 1):

        @pl.when(to_mates[i])
        def _():
            to_mate(i).wait_send()

    swap(True)[1].wait_send()
    for use, to, i, k in sends:

        @pl.when(use)
        def _():
            remote(m2, state_in.at[k], m2_s.at[i], m2_r.at[k], to).wait_send()


def per_device(seq_size, x_in, gate_in, b_in, c_in, log_decay, w_out):
    rows, columns = x_in.shape
    states = b_in.shape[1]
    depth = NY * NC * columns
    dma = pltpu.SemaphoreType.DMA
    vmem = pl.BlockSpec(memory_space=pltpu.VMEM)
    return pl.pallas_call(
        functools.partial(kernel, seq_size),
        out_shape=pltpu.VMEM((rows, columns), BF16),
        in_specs=[pl.BlockSpec(memory_space=pltpu.HBM)] * 6,
        out_specs=vmem,
        scratch_shapes=[
            pltpu.VMEM((rows, columns), BF16),
            pltpu.VMEM((rows, columns), BF16),
            pltpu.VMEM((rows, states), BF16),
            pltpu.VMEM((rows, states), BF16),
            pltpu.VMEM(log_decay.shape, F32),
            pltpu.VMEM((SPAN, states + 16, columns), BF16),
            pltpu.VMEM((states + 16, columns), BF16),
            pltpu.VMEM((3, states + 16, columns), BF16),
            pltpu.VMEM((states, columns), F32),
            pltpu.VMEM((rows, columns), F32),
            pltpu.VMEM((rows, columns), F32),
            pltpu.VMEM((NY * NC, rows, columns), BF16),
            pltpu.VMEM((NX, depth, columns), BF16),
            pltpu.VMEM((rows, columns), F32),
            pltpu.VMEM((NX - 1, rows, columns), BF16),
            pltpu.VMEM((NX - 1, rows, columns), BF16),
            dma((SPAN - 1,)),
            dma((SPAN - 1,)),
            dma((SPAN,)),
            dma((3,)),
            pltpu.SemaphoreType.REGULAR((SPAN,)),
            dma((NX - 1,)),
            dma((NX - 1,)),
            dma(()),
            dma(()),
            dma(()),
            dma((5,)),
            dma((CHUNKS, 2, NY // 2)),
            dma((CHUNKS, 2, NY // 2)),
            dma((CHUNKS, NY)),
            dma((CHUNKS, NY)),
            dma((NX - 1, CHUNKS)),
            dma((NX - 1, CHUNKS)),
        ],
        compiler_params=pltpu.CompilerParams(
            collective_id=0, has_side_effects=True, vmem_limit_bytes=56 * 2**20
        ),
        name="ssd_layer",
    )(x_in, gate_in, b_in, c_in, log_decay, w_out)


def solution(mesh):
    in_specs = (
        P("seq", "head"),
        P("seq", "head"),
        P("seq", None),
        P("seq", None),
        P("head", "seq"),
        P(None, "head"),
    )
    return jax.shard_map(
        functools.partial(per_device, mesh.shape["seq"]),
        mesh=mesh,
        in_specs=in_specs,
        out_specs=P("seq", "head"),
        check_vma=False,
    )
```

```python
import functools

import jax
import jax.numpy as jnp
from jax import lax
from jax.experimental import pallas as pl
from jax.experimental.pallas import tpu as pltpu
from jax.sharding import PartitionSpec as P

MESH = pl.DeviceIdType.MESH
BLOCK = 256
NX, NY, NC = 4, 8, 2
SPAN = 4
CHUNKS = 4
NT = (((1,), (1,)), ((), ()))
TN = (((0,), (0,)), ((), ()))
F32 = jnp.float32
BF16 = jnp.bfloat16


def exact(a, b):
    return lax.dot_general(a, b, NT, precision=lax.Precision.HIGHEST, preferred_element_type=F32)


def pack(ref, state, total):
    n = state.shape[0]
    row = lax.broadcasted_iota(jnp.int32, (16, state.shape[1]), 0)
    high = total.astype(BF16).astype(F32)
    tail = jnp.where(row == 0, high, jnp.where(row == 1, total - high, 0.0))
    ref[0:n, :] = state.astype(BF16)
    ref[n : n + 16, :] = tail.astype(BF16)


def unpack(ref, n):
    tail = ref[n : n + 16, :].astype(F32)
    return ref[0:n, :].astype(F32), tail[0:1] + tail[1:2]


def kernel(
    seq_size,
    x_hbm,
    gate_hbm,
    b_hbm,
    c_hbm,
    decay_hbm,
    w_ref,
    out_ref,
    x_ref,
    gate_ref,
    b_ref,
    c_ref,
    decay_ref,
    own_state,
    m2,
    state_in,
    start_ref,
    diag,
    wide,
    blocks,
    w_buf,
    total,
    part,
    part_in,
    m1_s,
    m1_r,
    m2_s,
    m2_r,
    ready,
    w_s,
    w_r,
    swap_s,
    swap_r,
    own_s,
    in_s,
    ring_s,
    ring_r,
    twin_s,
    twin_r,
    part_s,
    part_r,
):
    rows, columns = x_ref.shape
    states = b_ref.shape[1]
    channels = columns // decay_ref.shape[0]
    step = rows // CHUNKS
    s = lax.axis_index("seq")
    head = lax.axis_index("head")
    px, py, core = head // (NY * NC), (head // NC) % NY, head % NC
    group, place, odd = s // SPAN, s % SPAN, s % 2
    groups = seq_size // SPAN
    opening = group == 0

    def device(z, x, y, c):
        return (z, (x * NY + y) * NC + c)

    mate = device(s + 1 - 2 * odd, px, py, core)
    def after(i):
        return device((s + i) % seq_size, px, py, core)

    mates = [device(group * SPAN + (place + i) % SPAN, px, py, core) for i in range(1, SPAN)]
    to_mates = [opening | (odd == 0) if i == 0 else opening for i in range(SPAN - 1)]
    from_mates = [
        (opening & (place >= i + 1)) | ((odd == 1) if i == 0 else False) for i in range(SPAN - 1)
    ]
    pair_end = (group > 0) & (place == 1)
    group_end = (group == 1) & (place == SPAN - 1)
    late_pair, late, closing = (group > 0) & (place >= 2), group > 0, group == groups - 1
    pair_from = device(group * SPAN + 1, px, py, core)
    group_from = device(2 * SPAN - 1, px, py, core)
    opening_from = device(place, px, py, core)
    peers = [(px + i) % NX for i in range(1, NX)]
    peer_ids = [device(s, p, py, core) for p in peers]
    up = device(s, px, (py + 1) % NY, core)
    down = device(s, px, (py + NY - 1) % NY, core)
    twin = device(s, px, py, 1 - core)

    def remote(src, dst, send, recv, to):
        return pltpu.make_async_remote_copy(
            src_ref=src, dst_ref=dst, send_sem=send, recv_sem=recv, device_id=to, device_id_type=MESH
        )

    loads = [
        pltpu.make_async_copy(src, dst, in_s.at[i])
        for i, (src, dst) in enumerate(
            (
                (decay_hbm, decay_ref),
                (b_hbm, b_ref),
                (x_hbm, x_ref),
                (c_hbm, c_ref),
                (gate_hbm, gate_ref),
            )
        )
    ]
    for load in loads:
        load.start()

    partners = peer_ids + [up, down, twin]
    barrier = pltpu.get_barrier_semaphore()

    def signal(sem, to):
        pl.semaphore_signal(sem, inc=1, device_id=to, device_id_type=MESH)

    for to in partners:
        signal(barrier, to)
    sends = [(opening, after(SPAN * i), i - 1, 2) for i in (1, 2)]
    sends += [(pair_end, after(i), i - 1, 0) for i in (1, 2)]
    sends += [(group_end, after(i), i - 1, 1) for i in (2, 1, 4, 3)]
    for use, to, _, _ in sends:

        @pl.when(use)
        def _():
            signal(barrier, to)

    @pl.when(opening)
    def _():
        for i in range(1, SPAN):
            signal(barrier, mates[i - 1])

    @pl.when(late)
    def _():
        signal(barrier, mate)

    greetings = jnp.where(opening, SPAN - 1, 2 + place // 2 + group // 2)
    sent = []
    depth = NY * NC * columns
    half = depth // 2
    opposite = (px + NX // 2) % NX

    def swap(mine):
        slot = w_buf.at[opposite, pl.ds((odd if mine else 1 - odd) * half, half)]
        return slot, remote(slot, slot, swap_s, swap_r, mate)

    def start_swap():
        slot, copy = swap(True)
        remote(slot, slot, w_s.at[1], w_r.at[1], peer_ids[1]).wait_recv()
        copy.start()

    own_w = pltpu.make_async_copy(w_ref.at[pl.ds(px * depth, depth), :], w_buf.at[px], own_s)
    own_w.start()
    t_of = lax.broadcasted_iota(jnp.int32, (BLOCK, BLOCK), 0)
    s_of = lax.broadcasted_iota(jnp.int32, (BLOCK, BLOCK), 1)
    lower = s_of <= t_of
    ones = jnp.where(lower, 1.0, 0.0)
    first_head = lax.broadcasted_iota(jnp.int32, (BLOCK, columns), 1) < channels
    first_row = lax.broadcasted_iota(jnp.int32, (columns, BLOCK), 0) < channels
    local, cum_last = [], []
    for load in loads[:3]:
        load.wait()
    for q in range(rows // BLOCK):
        if q == 1:
            pl.semaphore_wait(barrier, len(partners) + greetings)

            @pl.when(late)
            def _():
                signal(ready.at[group - 1], opening_from)

            @pl.when(late_pair)
            def _():
                signal(ready.at[place - 2], pair_from)

            @pl.when(closing)
            def _():
                signal(ready.at[place], group_from)

            for i in (1, 0, 2):
                at, n = (odd * half, half) if i == 1 else (0, depth)
                copy = remote(
                    w_ref.at[pl.ds(peers[i] * depth + at, n), :],
                    w_buf.at[px, pl.ds(at, n)],
                    w_s.at[i],
                    w_r.at[i],
                    peer_ids[i],
                )
                copy.start()
                sent.append(copy)
        at = slice(q * BLOCK, (q + 1) * BLOCK)
        decay = decay_ref[:, at]
        cum = exact(ones, jnp.where(first_row, decay[0:1], decay[1:2]))
        wide[at, :] = cum
        last = cum[BLOCK - 1 :, :]
        to_end = jnp.exp(last - cum)
        b = b_ref[at, :].astype(F32)
        x = x_ref[at, :]
        halves = [
            lax.dot_general(
                (b * to_end[:, h * channels : h * channels + 1]).astype(BF16),
                x,
                TN,
                preferred_element_type=F32,
            )
            for h in range(2)
        ]
        local.append(jnp.where(first_head[:states], halves[0], halves[1]))
        cum_last.append(last)
    pack(
        own_state.at[place],
        local[0] * jnp.exp(cum_last[1]) + local[1],
        jnp.exp(cum_last[0] + cum_last[1]),
    )

    def to_mate(i):
        slot = own_state.at[place]
        return remote(slot, slot, m1_s.at[i], m1_r.at[i], mates[i])

    for i in range(SPAN - 1):

        @pl.when(to_mates[i])
        def _():
            to_mate(i).start()

    for load in loads[3:]:
        load.wait()
    for q in range(rows // BLOCK):
        at = slice(q * BLOCK, (q + 1) * BLOCK)
        decay = decay_ref[:, at]
        cum = wide[at, :]
        x = x_ref[at, :]
        scores = lax.dot_general(c_ref[at, :], b_ref[at, :], NT, preferred_element_type=F32)
        along = exact(jnp.where(first_row[56:72], decay[0:1], decay[1:2]), ones)
        halves = []
        for h in range(2):
            gap = cum[:, h * channels : h * channels + 1] - along[8 * h : 8 * h + 1, :]
            weights = jnp.where(lower, scores * jnp.exp(jnp.where(lower, gap, 0.0)), 0.0)
            halves.append(jnp.dot(weights.astype(BF16), x, preferred_element_type=F32))
        gate = gate_ref[at, :].astype(F32)
        gate = gate / (1.0 + jnp.exp(-gate))
        diag[at, :] = jnp.where(first_head, halves[0], halves[1]) * gate
        wide[at, :] = jnp.exp(cum) * gate

    def send(chosen):
        for use, to, i, k in chosen:

            @pl.when(use)
            def _():
                pl.semaphore_wait(ready.at[i], 1)
                remote(m2, state_in.at[k], m2_s.at[i], m2_r.at[k], to).start()

    def state_from(k):
        remote(m2, state_in.at[k], m2_s.at[0], m2_r.at[k], mate).wait_recv()
        return unpack(state_in.at[k], states)

    def wait_mates(chosen):
        for i in range(SPAN - 1):

            @pl.when(chosen[i])
            def _():
                slot = own_state.at[(place + SPAN - 1 - i) % SPAN]
                remote(slot, slot, m1_s.at[i], m1_r.at[i], mates[i]).wait_recv()

    wait_mates(from_mates)

    @pl.when(opening)
    def _():
        start_ref[...] = jnp.zeros_like(start_ref)

    for i in range(SPAN - 1):

        @pl.when(opening & (place > i))
        def _():
            more, its_decay = unpack(own_state.at[i], states)
            start_ref[...] = start_ref[...] * its_decay + more

    def send_total(use):
        @pl.when(use)
        def _():
            state, decay = unpack(own_state.at[0], states)
            for i in range(1, SPAN):
                more, its_decay = unpack(own_state.at[i], states)
                state, decay = state * its_decay + more, decay * its_decay
            pack(m2, state, decay)

        send([(use, to, i, k) for _, to, i, k in sends[:1]])

    send_total(opening & (place == SPAN - 1))

    def joined():
        state, decay = unpack(own_state.at[place], states)
        more, its_decay = unpack(own_state.at[jnp.maximum(place - 1, 0)], states)
        return more * decay + state, decay * its_decay

    @pl.when(pair_end)
    def _():
        pack(m2, *joined())

    send(sends[2:4])

    @pl.when(group_end)
    def _():
        state, decay = joined()
        more, its_decay = state_from(0)
        pack(m2, more * decay + state, decay * its_decay)

    send(sends[4:])

    @pl.when(late)
    def _():
        start_ref[...] = state_from(2)[0]

    @pl.when(closing)
    def _():
        more, its_decay = state_from(1)
        start_ref[...] = start_ref[...] * its_decay + more

    @pl.when(late_pair & jnp.logical_not(group_end))
    def _():
        state_from(0)

    @pl.when(late_pair)
    def _():
        more, its_decay = unpack(state_in.at[0], states)
        start_ref[...] = start_ref[...] * its_decay + more

    @pl.when(late & (odd == 1))
    def _():
        more, its_decay = unpack(own_state.at[jnp.maximum(place - 1, 0)], states)
        start_ref[...] = start_ref[...] * its_decay + more

    start = start_ref[...]
    starts = [start, start * jnp.exp(cum_last[0]) + local[0]]

    mine = py * NC + core
    for r in range(CHUNKS):
        at = slice(r * step, (r + 1) * step)
        start_bf = starts[r * step // BLOCK].astype(BF16)
        carry = jnp.dot(c_ref[at, :], start_bf, preferred_element_type=F32)
        blocks[mine, at, :] = (diag[at, :] + carry * wide[at, :]).astype(BF16)
        here = blocks.at[mine, at]
        for d, to in enumerate((up, down)):
            copy = remote(here, here, ring_s.at[r, d, 0], ring_r.at[r, d, 0], to)
            copy.start()
            sent.append(copy)
        copy = remote(here, here, twin_s.at[r, 0], twin_r.at[r, 0], twin)
        copy.start()
        sent.append(copy)

    wait_mates([opening & (place < i + 1) for i in range(SPAN - 1)])
    send_total(opening & (place < SPAN - 1))
    send(sends[1:2])

    def hops(r, d):
        return NY // 2 if (r + d) % 2 == 0 else NY // 2 - 1

    def behind(hop, d):
        return (py + NY - hop) % NY if d == 0 else (py + hop) % NY

    def wait_w():
        own_w.wait()
        for i in (0, 2):
            slot = w_buf.at[(px + NX - 1 - i) % NX]
            remote(slot, slot, w_s.at[i], w_r.at[i], peer_ids[i]).wait_recv()
        swap(False)[1].wait_recv()

    def product(r):
        at = slice(r * step, (r + 1) * step)
        for which in range(NY):
            if which == 0:
                where = py
            elif which < NY - 1:
                where = behind((which + 1) // 2, (which + 1) % 2)
            else:
                where = (py + NY // 2) % NY
            there = blocks.at[where * NC + 1 - core, at]
            remote(there, there, twin_s.at[r, which], twin_r.at[r, which], twin).wait_recv()
        gathered = jnp.concatenate([blocks[k, at, :] for k in range(NY * NC)], axis=1)
        for pair in ((1, 0), (2, None)):
            ws = [w_buf[px if i is None else peers[i]] for i in pair]
            both = jnp.dot(gathered, jnp.concatenate(ws, axis=1), preferred_element_type=F32)
            for k, i in enumerate(pair):
                value = both[:, k * columns : (k + 1) * columns]
                if i is None:
                    total[at, :] = value
                    continue
                part[i, at, :] = value.astype(BF16)
                copy = remote(
                    part.at[i, at], part_in.at[i, at], part_s.at[i, r], part_r.at[i, r], peer_ids[i]
                )
                copy.start()
                sent.append(copy)

    for hop in range(1, NY // 2 + 1):
        if hop == 2:

            start_swap()

        for r in range(CHUNKS):
            at = slice(r * step, (r + 1) * step)
            arrived = []
            for d, to in enumerate((up, down)):
                if hop > hops(r, d):
                    continue
                here = blocks.at[behind(hop, d) * NC + core, at]
                remote(here, here, ring_s.at[r, d, hop - 1], ring_r.at[r, d, hop - 1], to).wait_recv()
                if hop < hops(r, d):
                    copy = remote(here, here, ring_s.at[r, d, hop], ring_r.at[r, d, hop], to)
                    copy.start()
                    sent.append(copy)
                arrived.append((d, here))
            for d, here in arrived:
                which = 2 * hop - 1 + d if hop < NY // 2 else NY - 1
                copy = remote(here, here, twin_s.at[r, which], twin_r.at[r, which], twin)
                copy.start()
                sent.append(copy)
            if hop == NY // 2 and r == 1:
                wait_w()
            if hop == NY // 2 and r >= 1:
                product(r - 1)
    product(CHUNKS - 1)
    for r in range(CHUNKS):
        at = slice(r * step, (r + 1) * step)
        for i, to in enumerate(peer_ids):
            remote(part.at[i, at], part_in.at[i, at], part_s.at[i, r], part_r.at[i, r], to).wait_recv()
        value = total[at, :]
        for i in range(NX - 1):
            value = value + part_in[i, at, :].astype(F32)
        out_ref[at, :] = value.astype(BF16)
    for copy in sent:
        copy.wait_send()

    for i in range(SPAN - 1):

        @pl.when(to_mates[i])
        def _():
            to_mate(i).wait_send()

    swap(True)[1].wait_send()
    for use, to, i, k in sends:

        @pl.when(use)
        def _():
            remote(m2, state_in.at[k], m2_s.at[i], m2_r.at[k], to).wait_send()


def per_device(seq_size, x_in, gate_in, b_in, c_in, log_decay, w_out):
    rows, columns = x_in.shape
    states = b_in.shape[1]
    depth = NY * NC * columns
    dma = pltpu.SemaphoreType.DMA
    vmem = pl.BlockSpec(memory_space=pltpu.VMEM)
    return pl.pallas_call(
        functools.partial(kernel, seq_size),
        out_shape=pltpu.VMEM((rows, columns), BF16),
        in_specs=[pl.BlockSpec(memory_space=pltpu.HBM)] * 6,
        out_specs=vmem,
        scratch_shapes=[
            pltpu.VMEM((rows, columns), BF16),
            pltpu.VMEM((rows, columns), BF16),
            pltpu.VMEM((rows, states), BF16),
            pltpu.VMEM((rows, states), BF16),
            pltpu.VMEM(log_decay.shape, F32),
            pltpu.VMEM((SPAN, states + 16, columns), BF16),
            pltpu.VMEM((states + 16, columns), BF16),
            pltpu.VMEM((3, states + 16, columns), BF16),
            pltpu.VMEM((states, columns), F32),
            pltpu.VMEM((rows, columns), F32),
            pltpu.VMEM((rows, columns), F32),
            pltpu.VMEM((NY * NC, rows, columns), BF16),
            pltpu.VMEM((NX, depth, columns), BF16),
            pltpu.VMEM((rows, columns), F32),
            pltpu.VMEM((NX - 1, rows, columns), BF16),
            pltpu.VMEM((NX - 1, rows, columns), BF16),
            dma((SPAN - 1,)),
            dma((SPAN - 1,)),
            dma((SPAN,)),
            dma((3,)),
            pltpu.SemaphoreType.REGULAR((SPAN,)),
            dma((NX - 1,)),
            dma((NX - 1,)),
            dma(()),
            dma(()),
            dma(()),
            dma((5,)),
            dma((CHUNKS, 2, NY // 2)),
            dma((CHUNKS, 2, NY // 2)),
            dma((CHUNKS, NY)),
            dma((CHUNKS, NY)),
            dma((NX - 1, CHUNKS)),
            dma((NX - 1, CHUNKS)),
        ],
        compiler_params=pltpu.CompilerParams(
            collective_id=0, has_side_effects=True, vmem_limit_bytes=56 * 2**20
        ),
        name="ssd_layer",
    )(x_in, gate_in, b_in, c_in, log_decay, w_out)


def solution(mesh):
    in_specs = (
        P("seq", "head"),
        P("seq", "head"),
        P("seq", None),
        P("seq", None),
        P("head", "seq"),
        P(None, "head"),
    )
    return jax.shard_map(
        functools.partial(per_device, mesh.shape["seq"]),
        mesh=mesh,
        in_specs=in_specs,
        out_specs=P("seq", "head"),
        check_vma=False,
    )
```

```python
import functools

import jax
import jax.numpy as jnp
from jax import lax
from jax.experimental import pallas as pl
from jax.experimental.pallas import tpu as pltpu
from jax.sharding import PartitionSpec as P

MESH = pl.DeviceIdType.MESH
BLOCK = 256
NX, NY, NC = 4, 8, 2
SPAN = 4
CHUNKS = 4
NT = (((1,), (1,)), ((), ()))
TN = (((0,), (0,)), ((), ()))
F32 = jnp.float32
BF16 = jnp.bfloat16


def exact(a, b):
    return lax.dot_general(a, b, NT, precision=lax.Precision.HIGHEST, preferred_element_type=F32)


def pack(ref, state, total):
    n = state.shape[0]
    row = lax.broadcasted_iota(jnp.int32, (16, state.shape[1]), 0)
    high = total.astype(BF16).astype(F32)
    tail = jnp.where(row == 0, high, jnp.where(row == 1, total - high, 0.0))
    ref[0:n, :] = state.astype(BF16)
    ref[n : n + 16, :] = tail.astype(BF16)


def unpack(ref, n):
    tail = ref[n : n + 16, :].astype(F32)
    return ref[0:n, :].astype(F32), tail[0:1] + tail[1:2]


def kernel(
    seq_size,
    x_hbm,
    gate_hbm,
    b_hbm,
    c_hbm,
    decay_hbm,
    w_ref,
    out_ref,
    x_ref,
    gate_ref,
    b_ref,
    c_ref,
    decay_ref,
    own_state,
    m2,
    state_in,
    start_ref,
    diag,
    wide,
    blocks,
    w_buf,
    total,
    part,
    part_in,
    m1_s,
    m1_r,
    m2_s,
    m2_r,
    ready,
    w_s,
    w_r,
    swap_s,
    swap_r,
    own_s,
    in_s,
    ring_s,
    ring_r,
    twin_s,
    twin_r,
    part_s,
    part_r,
):
    rows, columns = x_ref.shape
    states = b_ref.shape[1]
    channels = columns // decay_ref.shape[0]
    step = rows // CHUNKS
    s = lax.axis_index("seq")
    head = lax.axis_index("head")
    px, py, core = head // (NY * NC), (head // NC) % NY, head % NC
    group, place, odd = s // SPAN, s % SPAN, s % 2
    groups = seq_size // SPAN
    opening = group == 0

    def device(z, x, y, c):
        return (z, (x * NY + y) * NC + c)

    mate = device(s + 1 - 2 * odd, px, py, core)
    def after(i):
        return device((s + i) % seq_size, px, py, core)

    mates = [device(group * SPAN + (place + i) % SPAN, px, py, core) for i in range(1, SPAN)]
    to_mates = [opening | (odd == 0) if i == 0 else opening for i in range(SPAN - 1)]
    from_mates = [
        (opening & (place >= i + 1)) | ((odd == 1) if i == 0 else False) for i in range(SPAN - 1)
    ]
    pair_end = (group > 0) & (place == 1)
    group_end = (group == 1) & (place == SPAN - 1)
    late_pair, late, closing = (group > 0) & (place >= 2), group > 0, group == groups - 1
    pair_from = device(group * SPAN + 1, px, py, core)
    group_from = device(2 * SPAN - 1, px, py, core)
    opening_from = device(place, px, py, core)
    peers = [(px + i) % NX for i in range(1, NX)]
    peer_ids = [device(s, p, py, core) for p in peers]
    up = device(s, px, (py + 1) % NY, core)
    down = device(s, px, (py + NY - 1) % NY, core)
    twin = device(s, px, py, 1 - core)

    def remote(src, dst, send, recv, to):
        return pltpu.make_async_remote_copy(
            src_ref=src, dst_ref=dst, send_sem=send, recv_sem=recv, device_id=to, device_id_type=MESH
        )

    loads = [
        pltpu.make_async_copy(src, dst, in_s.at[i])
        for i, (src, dst) in enumerate(
            (
                (decay_hbm, decay_ref),
                (b_hbm, b_ref),
                (x_hbm, x_ref),
                (c_hbm, c_ref),
                (gate_hbm, gate_ref),
            )
        )
    ]
    for load in loads:
        load.start()

    partners = peer_ids + [up, down, twin]
    barrier = pltpu.get_barrier_semaphore()

    def signal(sem, to):
        pl.semaphore_signal(sem, inc=1, device_id=to, device_id_type=MESH)

    for to in partners:
        signal(barrier, to)
    sends = [(opening, after(SPAN * i), i - 1, 2) for i in (1, 2)]
    sends += [(pair_end, after(i), i - 1, 0) for i in (1, 2)]
    sends += [(group_end, after(i), i - 1, 1) for i in (2, 1, 4, 3)]
    for use, to, _, _ in sends:

        @pl.when(use)
        def _():
            signal(barrier, to)

    @pl.when(opening)
    def _():
        for i in range(1, SPAN):
            signal(barrier, mates[i - 1])

    @pl.when(late)
    def _():
        signal(barrier, mate)

    greetings = jnp.where(opening, SPAN - 1, 2 + place // 2 + group // 2)
    sent = []
    depth = NY * NC * columns
    half = depth // 2
    opposite = (px + NX // 2) % NX

    def swap(mine):
        slot = w_buf.at[opposite, pl.ds((odd if mine else 1 - odd) * half, half)]
        return slot, remote(slot, slot, swap_s, swap_r, mate)

    def start_swap():
        slot, copy = swap(True)
        remote(slot, slot, w_s.at[1], w_r.at[1], peer_ids[1]).wait_recv()
        copy.start()

    t_of = lax.broadcasted_iota(jnp.int32, (BLOCK, BLOCK), 0)
    s_of = lax.broadcasted_iota(jnp.int32, (BLOCK, BLOCK), 1)
    lower = s_of <= t_of
    ones = jnp.where(lower, 1.0, 0.0)
    first_head = lax.broadcasted_iota(jnp.int32, (BLOCK, columns), 1) < channels
    first_row = lax.broadcasted_iota(jnp.int32, (columns, BLOCK), 0) < channels
    local, cum_last = [], []
    for load in loads[:3]:
        load.wait()
    for q in range(rows // BLOCK):
        if q == 1:
            pl.semaphore_wait(barrier, len(partners) + greetings)

            @pl.when(late)
            def _():
                signal(ready.at[group - 1], opening_from)

            @pl.when(late_pair)
            def _():
                signal(ready.at[place - 2], pair_from)

            @pl.when(closing)
            def _():
                signal(ready.at[place], group_from)

            for i in (1, 0, 2):
                at, n = (odd * half, half) if i == 1 else (0, depth)
                copy = remote(
                    w_ref.at[pl.ds(peers[i] * depth + at, n), :],
                    w_buf.at[px, pl.ds(at, n)],
                    w_s.at[i],
                    w_r.at[i],
                    peer_ids[i],
                )
                copy.start()
                sent.append(copy)
        at = slice(q * BLOCK, (q + 1) * BLOCK)
        decay = decay_ref[:, at]
        cum = exact(ones, jnp.where(first_row, decay[0:1], decay[1:2]))
        wide[at, :] = cum
        last = cum[BLOCK - 1 :, :]
        to_end = jnp.exp(last - cum)
        b = b_ref[at, :].astype(F32)
        x = x_ref[at, :]
        halves = [
            lax.dot_general(
                (b * to_end[:, h * channels : h * channels + 1]).astype(BF16),
                x,
                TN,
                preferred_element_type=F32,
            )
            for h in range(2)
        ]
        local.append(jnp.where(first_head[:states], halves[0], halves[1]))
        cum_last.append(last)
    pack(
        own_state.at[place],
        local[0] * jnp.exp(cum_last[1]) + local[1],
        jnp.exp(cum_last[0] + cum_last[1]),
    )

    def to_mate(i):
        slot = own_state.at[place]
        return remote(slot, slot, m1_s.at[i], m1_r.at[i], mates[i])

    for i in range(SPAN - 1):

        @pl.when(to_mates[i])
        def _():
            to_mate(i).start()

    own_w = pltpu.make_async_copy(w_ref.at[pl.ds(px * depth, depth), :], w_buf.at[px], own_s)
    own_w.start()
    for load in loads[3:]:
        load.wait()
    for q in range(rows // BLOCK):
        at = slice(q * BLOCK, (q + 1) * BLOCK)
        decay = decay_ref[:, at]
        cum = wide[at, :]
        x = x_ref[at, :]
        scores = lax.dot_general(c_ref[at, :], b_ref[at, :], NT, preferred_element_type=F32)
        along = exact(jnp.where(first_row[56:72], decay[0:1], decay[1:2]), ones)
        halves = []
        for h in range(2):
            gap = cum[:, h * channels : h * channels + 1] - along[8 * h : 8 * h + 1, :]
            weights = jnp.where(lower, scores * jnp.exp(jnp.where(lower, gap, 0.0)), 0.0)
            halves.append(jnp.dot(weights.astype(BF16), x, preferred_element_type=F32))
        gate = gate_ref[at, :].astype(F32)
        gate = gate / (1.0 + jnp.exp(-gate))
        diag[at, :] = jnp.where(first_head, halves[0], halves[1]) * gate
        wide[at, :] = jnp.exp(cum) * gate

    def send(chosen):
        for use, to, i, k in chosen:

            @pl.when(use)
            def _():
                pl.semaphore_wait(ready.at[i], 1)
                remote(m2, state_in.at[k], m2_s.at[i], m2_r.at[k], to).start()

    def state_from(k):
        remote(m2, state_in.at[k], m2_s.at[0], m2_r.at[k], mate).wait_recv()
        return unpack(state_in.at[k], states)

    def wait_mates(chosen):
        for i in range(SPAN - 1):

            @pl.when(chosen[i])
            def _():
                slot = own_state.at[(place + SPAN - 1 - i) % SPAN]
                remote(slot, slot, m1_s.at[i], m1_r.at[i], mates[i]).wait_recv()

    wait_mates(from_mates)

    @pl.when(opening)
    def _():
        start_ref[...] = jnp.zeros_like(start_ref)

    for i in range(SPAN - 1):

        @pl.when(opening & (place > i))
        def _():
            more, its_decay = unpack(own_state.at[i], states)
            start_ref[...] = start_ref[...] * its_decay + more

    def send_total(use):
        @pl.when(use)
        def _():
            state, decay = unpack(own_state.at[0], states)
            for i in range(1, SPAN):
                more, its_decay = unpack(own_state.at[i], states)
                state, decay = state * its_decay + more, decay * its_decay
            pack(m2, state, decay)

        send([(use, to, i, k) for _, to, i, k in sends[:1]])

    send_total(opening & (place == SPAN - 1))

    def joined():
        state, decay = unpack(own_state.at[place], states)
        more, its_decay = unpack(own_state.at[jnp.maximum(place - 1, 0)], states)
        return more * decay + state, decay * its_decay

    @pl.when(pair_end)
    def _():
        pack(m2, *joined())

    send(sends[2:4])

    @pl.when(group_end)
    def _():
        state, decay = joined()
        more, its_decay = state_from(0)
        pack(m2, more * decay + state, decay * its_decay)

    send(sends[4:])

    @pl.when(late)
    def _():
        start_ref[...] = state_from(2)[0]

    @pl.when(closing)
    def _():
        more, its_decay = state_from(1)
        start_ref[...] = start_ref[...] * its_decay + more

    @pl.when(late_pair & jnp.logical_not(group_end))
    def _():
        state_from(0)

    @pl.when(late_pair)
    def _():
        more, its_decay = unpack(state_in.at[0], states)
        start_ref[...] = start_ref[...] * its_decay + more

    @pl.when(late & (odd == 1))
    def _():
        more, its_decay = unpack(own_state.at[jnp.maximum(place - 1, 0)], states)
        start_ref[...] = start_ref[...] * its_decay + more

    start = start_ref[...]
    starts = [start, start * jnp.exp(cum_last[0]) + local[0]]

    mine = py * NC + core
    for r in range(CHUNKS):
        at = slice(r * step, (r + 1) * step)
        start_bf = starts[r * step // BLOCK].astype(BF16)
        carry = jnp.dot(c_ref[at, :], start_bf, preferred_element_type=F32)
        blocks[mine, at, :] = (diag[at, :] + carry * wide[at, :]).astype(BF16)
        here = blocks.at[mine, at]
        for d, to in enumerate((up, down)):
            copy = remote(here, here, ring_s.at[r, d, 0], ring_r.at[r, d, 0], to)
            copy.start()
            sent.append(copy)
        copy = remote(here, here, twin_s.at[r, 0], twin_r.at[r, 0], twin)
        copy.start()
        sent.append(copy)

    wait_mates([opening & (place < i + 1) for i in range(SPAN - 1)])
    send_total(opening & (place < SPAN - 1))
    send(sends[1:2])

    def hops(r, d):
        return NY // 2 if (r + d) % 2 == 0 else NY // 2 - 1

    def behind(hop, d):
        return (py + NY - hop) % NY if d == 0 else (py + hop) % NY

    def wait_w():
        own_w.wait()
        for i in (0, 2):
            slot = w_buf.at[(px + NX - 1 - i) % NX]
            remote(slot, slot, w_s.at[i], w_r.at[i], peer_ids[i]).wait_recv()
        swap(False)[1].wait_recv()

    def product(r):
        at = slice(r * step, (r + 1) * step)
        for which in range(NY):
            if which == 0:
                where = py
            elif which < NY - 1:
                where = behind((which + 1) // 2, (which + 1) % 2)
            else:
                where = (py + NY // 2) % NY
            there = blocks.at[where * NC + 1 - core, at]
            remote(there, there, twin_s.at[r, which], twin_r.at[r, which], twin).wait_recv()
        gathered = jnp.concatenate([blocks[k, at, :] for k in range(NY * NC)], axis=1)
        for pair in ((1, 0), (2, None)):
            ws = [w_buf[px if i is None else peers[i]] for i in pair]
            both = jnp.dot(gathered, jnp.concatenate(ws, axis=1), preferred_element_type=F32)
            for k, i in enumerate(pair):
                value = both[:, k * columns : (k + 1) * columns]
                if i is None:
                    total[at, :] = value
                    continue
                part[i, at, :] = value.astype(BF16)
                copy = remote(
                    part.at[i, at], part_in.at[i, at], part_s.at[i, r], part_r.at[i, r], peer_ids[i]
                )
                copy.start()
                sent.append(copy)

    for hop in range(1, NY // 2 + 1):
        if hop == 2:

            start_swap()

        for r in range(CHUNKS):
            at = slice(r * step, (r + 1) * step)
            arrived = []
            for d, to in enumerate((up, down)):
                if hop > hops(r, d):
                    continue
                here = blocks.at[behind(hop, d) * NC + core, at]
                remote(here, here, ring_s.at[r, d, hop - 1], ring_r.at[r, d, hop - 1], to).wait_recv()
                if hop < hops(r, d):
                    copy = remote(here, here, ring_s.at[r, d, hop], ring_r.at[r, d, hop], to)
                    copy.start()
                    sent.append(copy)
                arrived.append((d, here))
            for d, here in arrived:
                which = 2 * hop - 1 + d if hop < NY // 2 else NY - 1
                copy = remote(here, here, twin_s.at[r, which], twin_r.at[r, which], twin)
                copy.start()
                sent.append(copy)
            if hop == NY // 2 and r == 1:
                wait_w()
            if hop == NY // 2 and r >= 1:
                product(r - 1)
    product(CHUNKS - 1)
    for r in range(CHUNKS):
        at = slice(r * step, (r + 1) * step)
        for i, to in enumerate(peer_ids):
            remote(part.at[i, at], part_in.at[i, at], part_s.at[i, r], part_r.at[i, r], to).wait_recv()
        value = total[at, :]
        for i in range(NX - 1):
            value = value + part_in[i, at, :].astype(F32)
        out_ref[at, :] = value.astype(BF16)
    for copy in sent:
        copy.wait_send()

    for i in range(SPAN - 1):

        @pl.when(to_mates[i])
        def _():
            to_mate(i).wait_send()

    swap(True)[1].wait_send()
    for use, to, i, k in sends:

        @pl.when(use)
        def _():
            remote(m2, state_in.at[k], m2_s.at[i], m2_r.at[k], to).wait_send()


def per_device(seq_size, x_in, gate_in, b_in, c_in, log_decay, w_out):
    rows, columns = x_in.shape
    states = b_in.shape[1]
    depth = NY * NC * columns
    dma = pltpu.SemaphoreType.DMA
    vmem = pl.BlockSpec(memory_space=pltpu.VMEM)
    return pl.pallas_call(
        functools.partial(kernel, seq_size),
        out_shape=pltpu.VMEM((rows, columns), BF16),
        in_specs=[pl.BlockSpec(memory_space=pltpu.HBM)] * 6,
        out_specs=vmem,
        scratch_shapes=[
            pltpu.VMEM((rows, columns), BF16),
            pltpu.VMEM((rows, columns), BF16),
            pltpu.VMEM((rows, states), BF16),
            pltpu.VMEM((rows, states), BF16),
            pltpu.VMEM(log_decay.shape, F32),
            pltpu.VMEM((SPAN, states + 16, columns), BF16),
            pltpu.VMEM((states + 16, columns), BF16),
            pltpu.VMEM((3, states + 16, columns), BF16),
            pltpu.VMEM((states, columns), F32),
            pltpu.VMEM((rows, columns), F32),
            pltpu.VMEM((rows, columns), F32),
            pltpu.VMEM((NY * NC, rows, columns), BF16),
            pltpu.VMEM((NX, depth, columns), BF16),
            pltpu.VMEM((rows, columns), F32),
            pltpu.VMEM((NX - 1, rows, columns), BF16),
            pltpu.VMEM((NX - 1, rows, columns), BF16),
            dma((SPAN - 1,)),
            dma((SPAN - 1,)),
            dma((SPAN,)),
            dma((3,)),
            pltpu.SemaphoreType.REGULAR((SPAN,)),
            dma((NX - 1,)),
            dma((NX - 1,)),
            dma(()),
            dma(()),
            dma(()),
            dma((5,)),
            dma((CHUNKS, 2, NY // 2)),
            dma((CHUNKS, 2, NY // 2)),
            dma((CHUNKS, NY)),
            dma((CHUNKS, NY)),
            dma((NX - 1, CHUNKS)),
            dma((NX - 1, CHUNKS)),
        ],
        compiler_params=pltpu.CompilerParams(
            collective_id=0, has_side_effects=True, vmem_limit_bytes=56 * 2**20
        ),
        name="ssd_layer",
    )(x_in, gate_in, b_in, c_in, log_decay, w_out)


def solution(mesh):
    in_specs = (
        P("seq", "head"),
        P("seq", "head"),
        P("seq", None),
        P("seq", None),
        P("head", "seq"),
        P(None, "head"),
    )
    return jax.shard_map(
        functools.partial(per_device, mesh.shape["seq"]),
        mesh=mesh,
        in_specs=in_specs,
        out_specs=P("seq", "head"),
        check_vma=False,
    )
```
